256 devices in a mesh: tower: 2 (over core), tile: 128 (over x, z, y).
Axes of the slice: x: 4, y: 4, z: 8, core: 2. Of those that a mesh axis runs over, the one named last changes fastest.
Arguments:
- embeddings: bfloat16 [2, 65536, 1024], P('tower', 'tile'), may hold values from -2 to 2
- loss_weights: bfloat16 [2, 65536], P('tower', 'tile'), may hold values from 0.25 to 2
- dataset_of_block: int32 [128], replicated, may hold values from 0 to 41, never falling along the last dimension, each value on 1 to 6 neighbouring positions
- logit_scale: float32 [42], replicated, may hold values from 4 to 16
Outputs:
- grads: float32 [2, 65536, 1024], P('tower', 'tile')
The draws below stay inside these ranges and needn't reach their ends.
Inputs may be any that keep to these rules, and one draw needn't show every extreme that they name: `dataset_of_block`: never falls along the blocks; each dataset covers 1 to 6 consecutive blocks, and one covers exactly 6.
All inputs are finite; a program needn't handle non-finite values.
Results may differ from the reference program's by a relative error of at most 0.0028.
Values may be sent and summed in bfloat16 or wider, within the bound.
A program may use at most 128 MiB of HBM per device.

```python
import math
import jax
import jax.numpy as jnp
import numpy as np
from jax import lax

D = 1024
BLK = 512
MOSTB = 6
NBLK = 128
ROWS = 65536
NDATA = 42


def draw_embeddings(key, part):
    key = jax.random.fold_in(key, 11)
    keys = jax.random.split(key, 11)
    audio = jax.random.normal(keys[0], (ROWS, D), jnp.float32)
    noise = jax.random.normal(keys[1], (ROWS, D), jnp.float32)
    lift = 0.2
    spread_a = jnp.exp(jax.random.uniform(keys[2], (ROWS, 1), jnp.float32, -0.7, 0.7))
    spread_v = jnp.exp(jax.random.uniform(keys[3], (ROWS, 1), jnp.float32, -0.7, 0.7))
    audio = 2.0 * audio * spread_a * D ** (-0.5)
    video = 0.2 * audio + 2.0 * noise * spread_v * D ** (-0.5)
    count = ROWS // BLK
    paths = jax.random.normal(keys[6], (4, D), jnp.float32) * D ** (-0.5)
    block_a = jax.random.normal(keys[7], (count, 4), jnp.float32)
    block_v = jax.random.normal(keys[8], (count, 4), jnp.float32)
    row_a = jax.random.normal(keys[9], (ROWS, 4), jnp.float32)
    row_v = jax.random.normal(keys[10], (ROWS, 4), jnp.float32)
    coef_a = jnp.repeat(block_a, BLK, axis=0) + 0.5 * row_a
    coef_v = jnp.repeat(block_v, BLK, axis=0) + 0.5 * row_v
    for number in range(4):
        audio = audio + lift * coef_a[:, number:number + 1] * paths[number][None, :]
        video = video + lift * coef_v[:, number:number + 1] * paths[number][None, :]
    return jnp.clip(jnp.stack([audio, video]), -2.0, 2.0).astype(jnp.bfloat16)


def block_levels(rng, extent, cuts, smallest, high):
    gain = 1.0
    for dim, shards_of in cuts:
        draws = jax.random.uniform(jax.random.fold_in(jax.random.fold_in(rng, 6), dim), (shards_of,), jnp.float32, smallest / len(cuts), high / len(cuts))
        gain = gain * jnp.repeat(jnp.exp(draws), extent[dim] // shards_of).reshape((-1,) + (1,) * (len(extent) - 1 - dim))
    return gain


def split_up(number_of, total, reach, lean):
    weights = [(1 << 20) // math.isqrt(standing ** lean) + 1 for standing in range(2, number_of + 1)]
    spare, holding = total - reach - (number_of - 1), [1] * (number_of - 1)
    while spare > 0:
        movable = [i for i in range(number_of - 1) if holding[i] < reach]
        whole, budget = sum([weights[i] for i in movable]), spare
        for i in movable:
            addition = min(reach - holding[i], max(1, budget * weights[i] // whole), spare)
            holding[i] = holding[i] + addition
            spare = spare - addition
    return np.array([reach] + holding)


def uneven_parts(own_key, number_of, total, limit, skew):
    if number_of == 2:
        one = jax.random.randint(own_key, (), max(1, total - limit), min(limit, total - 1) + 1)
        return jnp.stack([one, total - one])
    tallies = jnp.asarray(split_up(number_of, total, limit, skew), jnp.int32)
    pairs = (number_of - 1) // 2
    giver, sink = tallies[1:1 + 2 * pairs:2], tallies[2:2 + 2 * pairs:2]
    slack = jnp.minimum(giver - 1, limit - sink)
    shifted = jax.random.randint(jax.random.fold_in(own_key, 1), (pairs,), 0, 1 << 20) % (slack + 1)
    tallies = tallies.at[1:1 + 2 * pairs:2].set(giver - shifted).at[2:2 + 2 * pairs:2].set(sink + shifted)
    return tallies[jax.random.permutation(jax.random.fold_in(own_key, 2), number_of)]


def setup_inputs(seed: int = 0) -> dict:
    arg_keys = jax.random.split(jax.random.key(seed), 5)
    embeddings = draw_embeddings(jax.random.fold_in(arg_keys[4], 71), 0)
    loss_weights = jnp.clip(0.25 + 1.75 * jax.random.uniform(arg_keys[1], (2, ROWS), jnp.float32) ** block_levels(arg_keys[1], (2, ROWS), ((0, 2), (1, 128)), -0.2, 0.2), 0.25, 2.0).astype(jnp.bfloat16)
    dataset_of_block = jnp.searchsorted(jnp.cumsum(uneven_parts(arg_keys[2], NDATA, NBLK, MOSTB, 2)), jnp.arange(NBLK), side="right").astype(jnp.int32)
    logit_scale = jnp.clip(jnp.exp(jax.random.uniform(arg_keys[3], (NDATA,), jnp.float32, math.log(4.0), math.log(16.0))), 4.0, 16.0)
    return {"embeddings": embeddings, "loss_weights": loss_weights, "dataset_of_block": dataset_of_block, "logit_scale": logit_scale}


def pick_value(table, index):
    return jnp.sum(jnp.where(jnp.arange(table.shape[0]) == index, table, jnp.zeros_like(table)))


def window_scores(mine, other_pad, ds_pad, dataset_of_block, logit_scale, index):
    span_rows = (2 * MOSTB - 1) * BLK
    queries = lax.dynamic_slice_in_dim(mine, (index * BLK).astype(jnp.int32), BLK, 0)
    keys = lax.dynamic_slice_in_dim(other_pad, (index * BLK).astype(jnp.int32), span_rows, 0)
    ident = lax.dynamic_slice_in_dim(ds_pad, index.astype(jnp.int32), 2 * MOSTB - 1, 0)
    own_set = pick_value(dataset_of_block, index)
    temper = jnp.sum(jnp.where(jnp.arange(logit_scale.shape[0]) == own_set, logit_scale, jnp.zeros_like(logit_scale)))
    grid = temper * jnp.dot(queries, keys.T, preferred_element_type=jnp.float32)
    present = jnp.repeat(ident == own_set, BLK)
    masked = jnp.where(present[None, :], grid, -jnp.inf)
    return masked, keys, temper


def lse_side(mine, other, dataset_of_block, logit_scale):
    margin = (MOSTB - 1) * BLK
    other_pad = jnp.pad(other, ((margin, margin), (0, 0)))
    ds_pad = jnp.pad(dataset_of_block, (MOSTB - 1, MOSTB - 1), constant_values=-1)

    def one_block(index):
        masked, keys, temper = window_scores(mine, other_pad, ds_pad, dataset_of_block, logit_scale, index)
        peak = jnp.max(masked, axis=1)
        return peak + jnp.log(jnp.sum(jnp.exp(masked - peak[:, None]), axis=1))

    blocks = lax.map(one_block, jnp.arange(dataset_of_block.shape[0], dtype=jnp.int32))
    return blocks.reshape(-1)


def grad_side(mine, other, weight_m, weight_o, lse_m, lse_o, dataset_of_block, logit_scale):
    margin = (MOSTB - 1) * BLK
    span_rows = (2 * MOSTB - 1) * BLK
    other_pad = jnp.pad(other, ((margin, margin), (0, 0)))
    ds_pad = jnp.pad(dataset_of_block, (MOSTB - 1, MOSTB - 1), constant_values=-1)
    lse_pad = jnp.pad(lse_o, (margin, margin))
    weight_pad = jnp.pad(weight_o, (margin, margin))
    columns = jnp.arange(span_rows, dtype=jnp.int32)
    rows_here = jnp.arange(BLK, dtype=jnp.int32)
    diagonal = columns[None, :] == rows_here[:, None] + margin

    def one_block(index):
        masked, keys, temper = window_scores(mine, other_pad, ds_pad, dataset_of_block, logit_scale, index)
        start = (index * BLK).astype(jnp.int32)
        lse_rows = lax.dynamic_slice_in_dim(lse_m, start, BLK, 0)
        weight_rows = lax.dynamic_slice_in_dim(weight_m, start, BLK, 0)
        weight_own = lax.dynamic_slice_in_dim(weight_o, start, BLK, 0)
        lse_cols = lax.dynamic_slice_in_dim(lse_pad, start, span_rows, 0)
        weight_cols = lax.dynamic_slice_in_dim(weight_pad, start, span_rows, 0)
        mass = weight_rows[:, None] * jnp.exp(masked - lse_rows[:, None]) + weight_cols[None, :] * jnp.exp(masked - lse_cols[None, :])
        mass = mass - jnp.where(diagonal, (weight_rows + weight_own)[:, None], jnp.zeros_like(mass))
        return temper * jnp.dot(mass.astype(jnp.bfloat16), keys, preferred_element_type=jnp.float32)

    blocks = lax.map(one_block, jnp.arange(dataset_of_block.shape[0], dtype=jnp.int32))
    return blocks.reshape(-1, mine.shape[1])


def reference(embeddings, loss_weights, dataset_of_block, logit_scale):
    audio = embeddings[0]
    video = embeddings[1]
    weight_a = loss_weights[0].astype(jnp.float32)
    weight_v = loss_weights[1].astype(jnp.float32)
    lse_a = lse_side(audio, video, dataset_of_block, logit_scale)
    lse_v = lse_side(video, audio, dataset_of_block, logit_scale)
    grad_a = grad_side(audio, video, weight_a, weight_v, lse_a, lse_v, dataset_of_block, logit_scale)
    grad_v = grad_side(video, audio, weight_v, weight_a, lse_v, lse_a, dataset_of_block, logit_scale)
    return jnp.stack([grad_a, grad_v])
```

```python
import jax
import jax.numpy as jnp
from jax import lax
from jax.experimental import pallas as pl
from jax.experimental.pallas import tpu as pltpu
from jax.sharding import PartitionSpec as P


MESH = pl.DeviceIdType.MESH
F32, BF16 = jnp.float32, jnp.bfloat16
BLK, D = 512, 1024
HALF = BLK // 2
COLS, LINES = 4, 32
NEG = -1e30
LOG2E = 1.4426950408889634
CH = 16

UNITS = 13


def kernel(ds_ref, scale_ref, x_ref, wt_ref, out_ref, held, score, mass, wts,
           row_m, row_l, col_m, col_l, lp, li, lf, lcol, mp, mi, mf,
           ya, yo, yi, zs, zr, zm, zo, zi, ends, edge,
           send, recv, s_in, s_mid, r_mid, s_out, r_out):
    t = lax.axis_index("tower")
    tile = lax.axis_index("tile")
    line, y = tile // COLS, tile % COLS
    sgn = 1 - 2 * (y // 2)
    far_k = 3 - 2 * (y // 2)

    def at(core, down, right):
        return (core, ((line + down + LINES) % LINES) * COLS + (y + right) % COLS)

    def rcopy(src, dst, ss, rs, dev):
        return pltpu.make_async_remote_copy(
            src_ref=src, dst_ref=dst, send_sem=ss, recv_sem=rs, device_id=dev, device_id_type=MESH)

    mate = at(1 - t, 0, 0)

    def arrived(ref, sem):
        rcopy(ref, ref, sem, sem, mate).wait_recv()

    barrier = pltpu.get_barrier_semaphore()
    peers = [mate]
    for core in (0, 1):
        for k in (1, 2, 3):
            peers.append(at(core, 0, k))
        for dz in (1, -1, 2, -2):
            peers.append(at(core, dz, 0))
    for dev in peers:
        pl.semaphore_signal(barrier, inc=1, device_id=dev, device_id_type=MESH)
    pl.semaphore_wait(barrier, len(peers))

    pending = []

    def go(copy):
        copy.start()
        pending.append(copy)
        return copy

    for j in (0, 1, 2):
        for g in (0, 1):
            right = (1 - t) * (j + 1)
            down = t * (1, -1, -2 * sgn)[j]
            unit = (1 - t) * (3 - j) + t * (6 + 2 * j + g)
            go(rcopy(x_ref.at[0, pl.ds(HALF * g, HALF)], held.at[unit], s_in.at[2 * j + g], recv.at[unit],
                     at(g, down, right)))
    for g in (0, 1):
        unit = (1 - t) * (12 - 12 * g) + t * (4 + g)
        go(rcopy(x_ref.at[0, pl.ds(HALF * g, HALF)], held.at[unit], s_in.at[6 + g], recv.at[unit], mate))
        mine = (1 - t) * (12 * g) + t * (4 + g)
        held[mine] = x_ref[0, HALF * g:HALF * g + HALF, :]
    wts[t] = jnp.broadcast_to(wt_ref[...].astype(F32), (8, BLK))
    go(rcopy(wts.at[t], wts.at[t], s_in.at[8], recv.at[13], mate))

    def block_of(down, right):
        return ds_ref[((line + down + LINES) % LINES) * COLS + (y + right) % COLS]

    def factors(k, b):
        mine = block_of(0, k)
        down = (0, -1, 1, 2 * sgn)[b]
        live = mine == block_of(down, 0)
        temper = scale_ref[mine] * LOG2E
        return jnp.where(live, temper, 0.0), jnp.where(live, 0.0, NEG)

    col_m[...] = jnp.full(col_m.shape, NEG, F32)
    col_l[...] = jnp.zeros(col_l.shape, F32)

    def video(b):
        return held[pl.ds(4 + 2 * b, 2)].reshape(BLK, D)

    def fold(k, blocks, slot):
        mults = [factors(k, b) for b in blocks]
        for b in blocks:
            at_score = 12 if b == 3 else 4 * b + k
            score[at_score] = lax.dot_general(held[k], video(b), (((1,), (1,)), ((), ())),
                                              preferred_element_type=F32)
        where_ = [12 if b == 3 else 4 * b + k for b in blocks]

        def rows(c, tops):
            at_rows = pl.ds(pl.multiple_of(c * CH, CH), CH)
            parts, peaks = [], []
            for n, b in enumerate(blocks):
                s = score[where_[n], at_rows, :] * mults[n][0] + mults[n][1]
                score[where_[n], at_rows, :] = s
                peaks.append(jnp.maximum(tops[n], jnp.maximum(s[0:8], s[8:16])))
                parts.extend([s[:, 128 * q:128 * q + 128] for q in range(4)])
            top = parts[0]
            for part in parts[1:]:
                top = jnp.maximum(top, part)
            total = jnp.exp2(parts[0] - top)
            for part in parts[1:]:
                total = total + jnp.exp2(part - top)
            row_m[slot, at_rows, :] = top
            row_l[slot, at_rows, :] = total
            return tuple(peaks)

        old = [col_m[b] for b in blocks]
        new = lax.fori_loop(0, HALF // CH, rows, tuple(old))

        def columns(c, sums):
            at_rows = pl.ds(pl.multiple_of(c * CH, CH), CH)
            result = []
            for n, b in enumerate(blocks):
                s = score[where_[n], at_rows, :]
                result.append(sums[n] + jnp.exp2(s[0:8] - new[n]) + jnp.exp2(s[8:16] - new[n]))
            return tuple(result)

        begin = tuple(col_l[b] * jnp.exp2(old[n] - new[n]) for n, b in enumerate(blocks))
        sums = lax.fori_loop(0, HALF // CH, columns, begin)
        for n, b in enumerate(blocks):
            col_m[b] = new[n]
            col_l[b] = sums[n]

    def forward(j):
        unit = 6 + 2 * j + t
        arrived(held.at[unit], recv.at[unit])
        go(rcopy(held.at[unit], held.at[unit], s_in.at[9 + j], recv.at[unit], mate))

    for g in (0, 1):
        unit = t * (12 - 12 * g) + (1 - t) * (4 + g)
        arrived(held.at[unit], recv.at[unit])
    arrived(wts.at[1 - t], recv.at[13])
    forward(0)
    forward(1)
    for j in (0, 1):
        unit = 6 + 2 * j + 1 - t
        arrived(held.at[unit], recv.at[unit])

    def one_unit(i, carry):
        k = i ^ (i // 2)

        @pl.when(k > 0)
        def _():
            arrived(held.at[k], recv.at[k])

        fold(k, (0, 1, 2), k)
        return carry

    lax.fori_loop(0, 3, one_unit, 0)
    forward(2)
    one_unit(3, 0)
    unit = 6 + 4 + 1 - t
    arrived(held.at[unit], recv.at[unit])
    fold(far_k, (3,), 4)

    lane = lax.broadcasted_iota(jnp.int32, (HALF, 128), 1)

    def pack_rows(k, carry):
        m, l = row_m[k], row_l[k]
        far_m = jnp.where(k == far_k, row_m[4], NEG)
        both = jnp.maximum(m, far_m)
        l = l * jnp.exp2(m - both) + row_l[4] * jnp.exp2(far_m - both)
        top = jnp.max(both, axis=1, keepdims=True)
        total = jnp.sum(l * jnp.exp2(both - top), axis=1, keepdims=True)
        lp[k] = jnp.where(lane == 0, top, total).T[0:8, :]
        return carry

    lax.fori_loop(0, 4, pack_rows, 0)
    for k in (1, 2, 3):
        go(rcopy(lp.at[k], li.at[k - 1], s_mid.at[k - 1], r_mid.at[k - 1], at(t, 0, k)))
    sub = lax.broadcasted_iota(jnp.int32, (8, BLK), 0)

    def pack_columns(b, carry):
        m, l = col_m[b], col_l[b]
        top = jnp.max(m, axis=0, keepdims=True)
        total = jnp.sum(l * jnp.exp2(m - top), axis=0, keepdims=True)
        mp[b] = jnp.where(sub == 0, top, total)
        return carry

    lax.fori_loop(0, 4, pack_columns, 0)
    go(rcopy(mp.at[0], mi.at[0], s_mid.at[3], r_mid.at[3], mate))
    for j in (0, 1, 2):
        for g in (0, 1):
            go(rcopy(mp.at[j + 1], mi.at[1 + 2 * j + t], s_mid.at[4 + 2 * j + g], r_mid.at[4 + 2 * j + t],
                     at(g, (-1, 1, 2 * sgn)[j], 0)))

    def merge(parts):
        tops = [p[0:1, :] for p in parts]
        top = tops[0]
        for other in tops[1:]:
            top = jnp.maximum(top, other)
        total = parts[0][1:2, :] * jnp.exp2(tops[0] - top)
        for n in range(1, len(parts)):
            total = total + parts[n][1:2, :] * jnp.exp2(tops[n] - top)
        return top + jnp.log(total) * LOG2E

    for k in (1, 2, 3):
        arrived(li.at[k - 1], r_mid.at[k - 1])
    w_half = wts[0, :, pl.ds(pl.multiple_of(HALF * t, HALF), HALF)][0:1, :]
    rows_lse = merge([lp[0]] + [li[k] for k in range(3)]) - jnp.log(w_half) * LOG2E
    lf[0] = jnp.broadcast_to(rows_lse, (8, HALF))
    for k in (1, 2, 3):
        go(rcopy(lf.at[0], lf.at[4 - k], s_mid.at[10 + k - 1], r_mid.at[10 + 4 - k - 1], at(t, 0, k)))
    for n in range(7):
        arrived(mi.at[n], r_mid.at[3 + n])
    cols_lse = merge([mp[0]] + [mi[n] for n in range(7)]) - jnp.log(wts[1][0:1, :]) * LOG2E
    mf[0] = jnp.broadcast_to(cols_lse, (8, BLK))
    for j in (0, 1, 2):
        go(rcopy(mf.at[0], mf.at[j + 1], s_mid.at[13 + j], r_mid.at[13 + j], at(t, (1, -1, -2 * sgn)[j], 0)))
    for k in (1, 2, 3):
        arrived(lf.at[k], r_mid.at[10 + k - 1])

    def turn(k, carry):
        lcol[k] = jnp.broadcast_to(lf[k][0:1, :], (128, HALF)).T
        return carry

    lax.fori_loop(0, 4, turn, 0)
    for j in (0, 1, 2):
        arrived(mf.at[j + 1], r_mid.at[13 + j])

    def derive(k, blocks):
        cols = [mf[b] for b in blocks]

        def rows(c, carry):
            at_rows = pl.ds(pl.multiple_of(c * CH, CH), CH)
            lse = lcol[k, at_rows, :]
            lse = jnp.concatenate([lse] * 4, axis=1)
            for n, b in enumerate(blocks):
                index = 12 if b == 3 else 4 * b + k
                s = score[index, at_rows, :]
                lse_c = jnp.concatenate([cols[n], cols[n]], axis=0)
                g = jnp.exp2(s - lse) + jnp.exp2(s - lse_c)
                if b == 0:
                    r_id = lax.broadcasted_iota(jnp.int32, (CH, BLK), 0) + c * CH + HALF * t + BLK * k
                    c_id = lax.broadcasted_iota(jnp.int32, (CH, BLK), 1)
                    both = jnp.concatenate([wts[0] + wts[1]] * 2, axis=0)
                    g = g - jnp.where(r_id == c_id, both, 0.0)
                mass[index, at_rows, :] = g.astype(BF16)
            return carry

        lax.fori_loop(0, HALF // CH, rows, 0)

    derive(far_k, (3,))
    edge[...] = jnp.dot(mass[12], video(3), preferred_element_type=F32)

    def row_grad(k):
        derive(k, (0, 1, 2))
        total = jnp.where(k == far_k, edge[...], 0.0)
        for b in (0, 1, 2):
            total = total + jnp.dot(mass[4 * b + k], video(b), preferred_element_type=F32)
        return total

    def outward(i, carry):
        k = 2 + i - 3 * (i // 2)
        yo[k - 1] = row_grad(k).astype(BF16)
        rcopy(yo.at[k - 1], yi.at[k - 1], s_out.at[k - 1], r_out.at[k - 1], at(t, 0, k)).start()
        return carry

    lax.fori_loop(0, 3, outward, 0)
    derive(0, (0, 1, 2))

    def col_grad(b, half):
        cols = pl.ds(pl.multiple_of(HALF * half, HALF), HALF)
        if b == 3:
            return lax.dot_general(mass[12, :, cols], held[far_k], (((0,), (0,)), ((), ())),
                                   preferred_element_type=F32)
        g = mass[4 * b:4 * b + 4, :, cols].reshape(4 * HALF, HALF)
        a = held[0:4].reshape(4 * HALF, D)
        return lax.dot_general(g, a, (((0,), (0,)), ((), ())), preferred_element_type=F32)

    for b in (3, 1, 2, 0):
        zs[b] = col_grad(b, 1 - t)
        go(rcopy(zs.at[b], zr.at[b], s_out.at[3 + b], r_out.at[3 + b], mate))
        zm[b] = col_grad(b, t)
    for b in (3, 1, 2):
        arrived(zr.at[b], r_out.at[3 + b])
        zo[b - 1] = (zm[b] + zr[b]).astype(BF16)
        go(rcopy(zo.at[b - 1], zi.at[b - 1], s_out.at[6 + b], r_out.at[6 + b], at(t, (0, -1, 1, 2 * sgn)[b], 0)))
    ya[...] = jnp.where(0 == far_k, edge[...], 0.0)
    for b in (0, 1, 2):
        ya[...] += jnp.dot(mass[4 * b], video(b), preferred_element_type=F32)

    temper = scale_ref[block_of(0, 0)]
    arrived(zr.at[0], r_out.at[3])
    for j in range(3):
        arrived(zi.at[j], r_out.at[7 + j])
    for k in range(3):
        arrived(yi.at[k], r_out.at[k])

    def finish(c, carry):
        at_rows = pl.ds(pl.multiple_of(c * CH, CH), CH)
        ga = ya[at_rows, :]
        gv = zm[0, at_rows, :] + zr[0, at_rows, :]
        for n in range(3):
            ga = ga + yi[n, at_rows, :].astype(F32)
            gv = gv + zi[n, at_rows, :].astype(F32)
        ends[0, at_rows, :] = temper * ga
        ends[1, at_rows, :] = temper * gv
        return carry

    lax.fori_loop(0, HALF // CH, finish, 0)
    half_rows = pl.ds(pl.multiple_of(HALF * t, HALF), HALF)
    other_rows = pl.ds(pl.multiple_of(HALF * (1 - t), HALF), HALF)
    go(rcopy(ends.at[1 - t], out_ref.at[0, half_rows], s_out.at[10], r_out.at[10], mate))
    out_ref[0, half_rows, :] = ends[t]
    arrived(out_ref.at[0, other_rows], r_out.at[10])
    for copy in pending:
        copy.wait_send()
    for k in (1, 2, 3):
        rcopy(yo.at[k - 1], yi.at[k - 1], s_out.at[k - 1], r_out.at[k - 1], at(t, 0, k)).wait_send()


def on_device(embeddings, loss_weights, dataset_of_block, logit_scale):
    vmem = pl.BlockSpec(memory_space=pltpu.VMEM)
    smem = pl.BlockSpec(memory_space=pltpu.SMEM)
    dma = pltpu.SemaphoreType.DMA
    scratch = [
        pltpu.VMEM((UNITS, HALF, D), BF16),
        pltpu.VMEM((13, HALF, BLK), F32),
        pltpu.VMEM((13, HALF, BLK), BF16),
        pltpu.VMEM((2, 8, BLK), F32),
        pltpu.VMEM((5, HALF, 128), F32),
        pltpu.VMEM((5, HALF, 128), F32),
        pltpu.VMEM((4, 8, BLK), F32),
        pltpu.VMEM((4, 8, BLK), F32),
        pltpu.VMEM((4, 8, HALF), F32),
        pltpu.VMEM((3, 8, HALF), F32),
        pltpu.VMEM((4, 8, HALF), F32),
        pltpu.VMEM((4, HALF, 128), F32),
        pltpu.VMEM((4, 8, BLK), F32),
        pltpu.VMEM((7, 8, BLK), F32),
        pltpu.VMEM((4, 8, BLK), F32),
        pltpu.VMEM((HALF, D), F32),
        pltpu.VMEM((3, HALF, D), BF16),
        pltpu.VMEM((3, HALF, D), BF16),
        pltpu.VMEM((4, HALF, D), F32),
        pltpu.VMEM((4, HALF, D), F32),
        pltpu.VMEM((4, HALF, D), F32),
        pltpu.VMEM((3, HALF, D), BF16),
        pltpu.VMEM((3, HALF, D), BF16),
        pltpu.VMEM((2, HALF, D), F32),
        pltpu.VMEM((HALF, D), F32),
        dma((1,)), dma((14,)), dma((12,)), dma((16,)), dma((16,)), dma((11,)), dma((11,)),
    ]
    return pl.pallas_call(
        kernel,
        out_shape=jax.ShapeDtypeStruct((1, BLK, D), F32),
        in_specs=[smem, smem, vmem, vmem],
        out_specs=vmem,
        scratch_shapes=scratch,
        compiler_params=pltpu.CompilerParams(
            collective_id=0, has_side_effects=True, vmem_limit_bytes=56 * 2**20),
    )(dataset_of_block, logit_scale, embeddings, loss_weights)


def solution(mesh):
    in_specs = (P("tower", "tile", None), P("tower", "tile"), P(), P())
    return jax.shard_map(
        on_device, mesh=mesh, in_specs=in_specs, out_specs=P("tower", "tile", None), check_vma=False)
```

```python
import jax
import jax.numpy as jnp
from jax import lax
from jax.experimental import pallas as pl
from jax.experimental.pallas import tpu as pltpu
from jax.sharding import PartitionSpec as P


MESH = pl.DeviceIdType.MESH
F32, BF16 = jnp.float32, jnp.bfloat16
BLK, D = 512, 1024
HALF, QUART = BLK // 2, BLK // 4
COLS, LINES = 4, 32
NEG = -1e30
LOG2E = 1.4426950408889634
CH = 16

UNITS = 12


def kernel(ds_ref, scale_ref, x_ref, wt_ref, out_ref, held, score, mass, wts,
           row_m, row_l, col_m, col_l, lp, li, lf, lcol, mp, mi, mf,
           ya, yp, yo, yi, yt, yr, xo, xi, zs, zr, zm, zo, zi, ends,
           s_in, r_in, s_held, r_held, s_mid, r_mid, s_out, r_out):
    t = lax.axis_index("tower")
    tile = lax.axis_index("tile")
    line, y = tile // COLS, tile % COLS
    sel = y // 2
    sgn = 1 - 2 * sel
    edge = y % 3 == 0
    edge_k = 3 - 2 * sel
    edge_b = 2 - sel

    def at(core, down, right):
        return (core, ((line + down + LINES) % LINES) * COLS + (y + right) % COLS)

    def rcopy(src, dst, ss, rs, dev):
        return pltpu.make_async_remote_copy(
            src_ref=src, dst_ref=dst, send_sem=ss, recv_sem=rs, device_id=dev, device_id_type=MESH)

    mate = at(1 - t, 0, 0)
    across = at(t, -sgn, edge_k)

    def arrived(ref, sem):
        rcopy(ref, ref, sem, sem, mate).wait_recv()

    barrier = pltpu.get_barrier_semaphore()
    peers = [mate, at(t, 0, 2)]
    for core in (0, 1):
        for k in (1, 3):
            peers.append(at(core, 0, k))
        for dz in (1, -1):
            peers.append(at(core, dz, 0))
    for dev in peers:
        pl.semaphore_signal(barrier, inc=1, device_id=dev, device_id_type=MESH)

    @pl.when(edge)
    def _():
        pl.semaphore_signal(barrier, inc=1, device_id=across, device_id_type=MESH)

    pl.semaphore_wait(barrier, len(peers) + edge.astype(jnp.int32))

    pending, edge_pending = [], []

    def go(copy):
        copy.start()
        pending.append(copy)

    def edge_go(copy):
        edge_pending.append(copy)

        @pl.when(edge)
        def _():
            copy.start()

    def drain():
        for copy in pending:
            copy.wait_send()

        @pl.when(edge)
        def _():
            for copy in edge_pending:
                copy.wait_send()

    def half(h):
        return pl.ds(QUART * h, QUART)

    for step in (0, 1):
        for way in (0, 1):
            h = step ^ way
            for g in (0, 1):
                sign = 1 - 2 * way
                unit = (1 - t) * (3 - 2 * way) + t * (6 + 2 * way + g)
                go(rcopy(x_ref.at[0, pl.ds(HALF * g + QUART * h, QUART)], held.at[unit, half(h)],
                         s_in.at[4 * step + 2 * way + g], r_held.at[unit, h], at(g, t * sign, (1 - t) * sign)))
    for g in (0, 1):
        unit = (1 - t) * (11 - 11 * g) + t * (4 + g)
        go(rcopy(x_ref.at[0, pl.ds(HALF * g, HALF)], held.at[unit], s_in.at[8 + g], r_held.at[unit, 0], mate))
        mine = (1 - t) * (11 * g) + t * (4 + g)
        held[mine] = x_ref[0, HALF * g:HALF * g + HALF, :]
    wts[t] = jnp.broadcast_to(wt_ref[...].astype(F32), (8, BLK))
    go(rcopy(wts.at[t], wts.at[t], s_in.at[10], r_in.at[0], mate))

    def block_of(down, right):
        return ds_ref[((line + down + LINES) % LINES) * COLS + (y + right) % COLS]

    def factors(mine, other):
        live = mine == other
        temper = scale_ref[mine] * LOG2E
        return jnp.where(live, temper, 0.0), jnp.where(live, 0.0, NEG)

    col_m[...] = jnp.full(col_m.shape, NEG, F32)
    col_l[...] = jnp.zeros(col_l.shape, F32)
    row_m[4] = jnp.full((HALF, 128), NEG, F32)
    row_l[4] = jnp.zeros((HALF, 128), F32)

    def video(b):
        return held[pl.ds(4 + 2 * b, 2)].reshape(BLK, D)

    def fold(unit, slot, blocks):
        for b, index, mult, off in blocks:
            score[index] = lax.dot_general(held[unit], video(b), (((1,), (1,)), ((), ())),
                                           preferred_element_type=F32)

        def rows(c, tops):
            at_rows = pl.ds(pl.multiple_of(c * CH, CH), CH)
            parts, peaks = [], []
            for n, (b, index, mult, off) in enumerate(blocks):
                s = score[index, at_rows, :] * mult + off
                score[index, at_rows, :] = s
                peaks.append(jnp.maximum(tops[n], jnp.maximum(s[0:8], s[8:16])))
                parts.extend([s[:, 128 * q:128 * q + 128] for q in range(4)])
            top = parts[0]
            for part in parts[1:]:
                top = jnp.maximum(top, part)
            total = jnp.exp2(parts[0] - top)
            for part in parts[1:]:
                total = total + jnp.exp2(part - top)
            row_m[slot, at_rows, :] = top
            row_l[slot, at_rows, :] = total
            return tuple(peaks)

        old = [col_m[b] for b, _, _, _ in blocks]
        new = lax.fori_loop(0, HALF // CH, rows, tuple(old))

        def columns(c, sums):
            at_rows = pl.ds(pl.multiple_of(c * CH, CH), CH)
            result = []
            for n, (b, index, mult, off) in enumerate(blocks):
                s = score[index, at_rows, :]
                result.append(sums[n] + jnp.exp2(s[0:8] - new[n]) + jnp.exp2(s[8:16] - new[n]))
            return tuple(result)

        begin = tuple(col_l[b] * jnp.exp2(old[n] - new[n]) for n, (b, _, _, _) in enumerate(blocks))
        sums = lax.fori_loop(0, HALF // CH, columns, begin)
        for n, (b, _, _, _) in enumerate(blocks):
            col_m[b] = new[n]
            col_l[b] = sums[n]

    def fold_unit(k):
        mine = block_of(0, k)
        fold(k, k, [(b, 4 * b + k) + factors(mine, block_of((0, -1, 1)[b], 0)) for b in (0, 1, 2)])

    for g in (0, 1):
        unit = t * (11 - 11 * g) + (1 - t) * (4 + g)
        arrived(held.at[unit], r_held.at[unit, 0])
    arrived(wts.at[1 - t], r_in.at[0])

    for unit, h, way in ((3, 0, 1), (1, 1, -1)):
        arrived(held.at[unit, half(h)], r_held.at[unit, h])
        go(rcopy(held.at[unit, half(h)], held.at[2, half(h)], s_held.at[h], r_held.at[2, h], at(t, 0, way)))
    for j in (0, 1):
        unit = 6 + 2 * j + t
        for h in (0, 1):
            arrived(held.at[unit, half(h)], r_held.at[unit, h])
        go(rcopy(held.at[unit], held.at[unit], s_held.at[2 + j], r_held.at[unit, 0], mate))
    for unit, h in ((3, 1), (1, 0)):
        arrived(held.at[unit, half(h)], r_held.at[unit, h])

    edge_go(rcopy(held.at[edge_k], held.at[10], s_held.at[4], r_held.at[10, 0], at(t, sgn, 0)))

    for j in (0, 1):
        unit = 6 + 2 * j + 1 - t
        arrived(held.at[unit], r_held.at[unit, 0])

    def one_unit(i, carry):
        k = i ^ (i // 2)

        @pl.when(k == 2)
        def _():
            for h in (0, 1):
                arrived(held.at[2, half(h)], r_held.at[2, h])

        fold_unit(k)
        return carry

    lax.fori_loop(0, 4, one_unit, 0)

    @pl.when(edge)
    def _():
        arrived(held.at[10], r_held.at[10, 0])
        fold(10, 4, [(edge_b, 12) + factors(block_of(-sgn, edge_k), block_of(sgn, 0))])

    sub = lax.broadcasted_iota(jnp.int32, (2, BLK), 0)

    def pack_columns(b, carry):
        m, l = col_m[b], col_l[b]
        top = jnp.max(m, axis=0, keepdims=True)
        total = jnp.sum(l * jnp.exp2(m - top), axis=0, keepdims=True)
        mp[b] = jnp.where(sub == 0, top, total)
        return carry

    lax.fori_loop(0, 3, pack_columns, 0)
    for j in (0, 1):
        for g in (0, 1):
            go(rcopy(mp.at[j + 1], mi.at[2 * j + t], s_mid.at[2 * j + g], r_mid.at[2 * j + t],
                     at(g, (-1, 1)[j], 0)))
    go(rcopy(mp.at[0], mi.at[4], s_mid.at[4], r_mid.at[4], mate))
    lane = lax.broadcasted_iota(jnp.int32, (HALF, 128), 1)

    def pack_rows(k, carry):
        m, l = row_m[k], row_l[k]
        top = jnp.max(m, axis=1, keepdims=True)
        total = jnp.sum(l * jnp.exp2(m - top), axis=1, keepdims=True)
        lp[k] = jnp.where(lane == 0, top, total).T[0:2, :]
        return carry

    lax.fori_loop(0, 5, pack_rows, 0)
    for k in (1, 2, 3):
        go(rcopy(lp.at[k], li.at[k - 1], s_mid.at[4 + k], r_mid.at[4 + k], at(t, 0, k)))
    li[3] = jnp.where(sub[:, 0:HALF] == 0, NEG, 0.0)

    edge_go(rcopy(lp.at[4], li.at[4], s_mid.at[8], r_mid.at[8], across))

    def merge(parts):
        tops = [p[0:1, :] for p in parts]
        top = tops[0]
        for other in tops[1:]:
            top = jnp.maximum(top, other)
        total = parts[0][1:2, :] * jnp.exp2(tops[0] - top)
        for n in range(1, len(parts)):
            total = total + parts[n][1:2, :] * jnp.exp2(tops[n] - top)
        return top + jnp.log(total) * LOG2E

    for n in range(5):
        arrived(mi.at[n], r_mid.at[n])
    mf[0] = merge([mp[0]] + [mi[n] for n in range(5)]) - jnp.log(wts[1][0:1, :]) * LOG2E
    for j in (0, 1):
        go(rcopy(mf.at[0], mf.at[j + 1], s_mid.at[9 + j], r_mid.at[9 + j], at(t, (1, -1)[j], 0)))
    for k in (1, 2, 3):
        arrived(li.at[k - 1], r_mid.at[4 + k])

    @pl.when(edge)
    def _():
        arrived(li.at[4], r_mid.at[8])
        li[3] = li[4]

    w_half = wts[0, :, pl.ds(pl.multiple_of(HALF * t, HALF), HALF)][0:1, :]
    lf[0] = merge([lp[0]] + [li[n] for n in range(4)]) - jnp.log(w_half) * LOG2E
    for k in (1, 2, 3):
        go(rcopy(lf.at[0], lf.at[4 - k], s_mid.at[10 + k], r_mid.at[10 + 4 - k], at(t, 0, k)))

    edge_go(rcopy(lf.at[0], lf.at[4], s_mid.at[14], r_mid.at[14], across))

    for k in (1, 2, 3):
        arrived(lf.at[k], r_mid.at[10 + k])

    def turn(k):
        lcol[k] = jnp.broadcast_to(lf[k], (128, HALF)).T

    for k in range(4):
        turn(k)
    for j in (0, 1):
        arrived(mf.at[j + 1], r_mid.at[9 + j])

    def derive(slot, blocks):
        cols = [jnp.broadcast_to(mf[b], (CH, BLK)) for b, _ in blocks]

        def rows(c, carry):
            at_rows = pl.ds(pl.multiple_of(c * CH, CH), CH)
            lse = jnp.concatenate([lcol[slot, at_rows, :]] * 4, axis=1)
            for n, (b, index) in enumerate(blocks):
                s = score[index, at_rows, :]
                g = jnp.exp2(s - lse) + jnp.exp2(s - cols[n])
                if isinstance(b, int) and b == 0:
                    r_id = lax.broadcasted_iota(jnp.int32, (CH, BLK), 0) + c * CH + HALF * t + BLK * slot
                    c_id = lax.broadcasted_iota(jnp.int32, (CH, BLK), 1)
                    both = jnp.concatenate([wts[0] + wts[1]] * 2, axis=0)
                    g = g - jnp.where(r_id == c_id, both, 0.0)
                mass[index, at_rows, :] = g.astype(BF16)
            return carry

        lax.fori_loop(0, HALF // CH, rows, 0)

    def derive_unit(k):
        derive(k, [(b, 4 * b + k) for b in (0, 1, 2)])

    def row_grad(k):
        total = jnp.dot(mass[k], video(0), preferred_element_type=F32)
        for b in (1, 2):
            total = total + jnp.dot(mass[4 * b + k], video(b), preferred_element_type=F32)
        return total

    first = sel

    def quarter(h):
        return pl.ds(pl.multiple_of(QUART * h, QUART), QUART)

    @pl.when(edge)
    def _():
        arrived(lf.at[4], r_mid.at[14])
        turn(4)
        derive(4, [(edge_b, 12)])
        xo[...] = jnp.dot(mass[12], video(edge_b), preferred_element_type=F32).astype(BF16)

    for h in (first, 1 - first):
        edge_go(rcopy(xo.at[quarter(h)], xi.at[quarter(h)], s_out.at[h], r_out.at[h], at(t, -sgn, 0)))

    derive_unit(2)
    yt[...] = row_grad(2).astype(BF16)
    for h, way in ((0, 1), (1, -1)):
        go(rcopy(yt.at[half(h)], yr.at[h], s_out.at[2 + h], r_out.at[2 + h], at(t, 0, way)))

    def derive_rest(i, carry):
        derive_unit(i + i // 2)
        return carry

    lax.fori_loop(0, 3, derive_rest, 0)

    def col_grad(into, b, part):
        cols = pl.ds(pl.multiple_of(HALF * part, HALF), HALF)
        g = mass[4 * b:4 * b + 4, :, cols].reshape(4 * HALF, HALF)
        a = held[0:4].reshape(4 * HALF, D)
        into[b] = lax.dot_general(g, a, (((0,), (0,)), ((), ())), preferred_element_type=F32)
        if b > 0:
            @pl.when(edge & (edge_b == b))
            def _():
                into[b] += lax.dot_general(mass[12, :, cols], held[10], (((0,), (0,)), ((), ())),
                                           preferred_element_type=F32)

    for b in (1, 2):
        col_grad(zs, b, 1 - t)
        go(rcopy(zs.at[b], zr.at[b], s_out.at[4 + b], r_out.at[4 + b], mate))
    for b in (1, 2):
        col_grad(zm, b, t)
    for b in (1, 2):
        arrived(zr.at[b], r_out.at[4 + b])
        zo[b - 1] = (zm[b] + zr[b]).astype(BF16)
        go(rcopy(zo.at[b - 1], zi.at[b - 1], s_out.at[6 + b], r_out.at[6 + b], at(t, (0, -1, 1)[b], 0)))
    for n, k in ((0, 1), (1, 3)):
        yp[n] = row_grad(k)

    def add_edge(h):
        @pl.when(edge)
        def _():
            arrived(xi.at[quarter(h)], r_out.at[h])
            yp[1 - sel, quarter(h)] += xi[quarter(h)].astype(F32)

    def send_on(n, h):
        yo[n, half(h)] = yp[n, half(h)].astype(BF16)
        go(rcopy(yo.at[n, half(h)], yi.at[n, half(h)], s_out.at[9 + 2 * n + h], r_out.at[9 + 2 * n + h],
                 at(t, 0, 1 - 2 * n)))

    add_edge(first)
    send_on(0, 1)
    send_on(1, 0)
    add_edge(1 - first)
    for n in (0, 1):
        arrived(yr.at[n], r_out.at[2 + n])
        yp[n, half(n)] += yr[n].astype(F32)
        send_on(n, n)

    ya[...] = row_grad(0)
    col_grad(zs, 0, 1 - t)
    go(rcopy(zs.at[0], zr.at[0], s_out.at[4], r_out.at[4], mate))
    col_grad(zm, 0, t)

    temper = scale_ref[block_of(0, 0)]
    half_rows = pl.ds(pl.multiple_of(HALF * t, HALF), HALF)
    other_rows = pl.ds(pl.multiple_of(HALF * (1 - t), HALF), HALF)

    def finish(mode, value):
        def rows(c, carry):
            at_rows = pl.ds(pl.multiple_of(c * CH, CH), CH)
            ends[mode, at_rows, :] = temper * value(at_rows)
            return carry

        lax.fori_loop(0, HALF // CH, rows, 0)

        @pl.when(t == mode)
        def _():
            out_ref[0, half_rows, :] = ends[mode]

        @pl.when(t != mode)
        def _():
            rcopy(ends.at[mode], out_ref.at[0, half_rows], s_out.at[13], r_out.at[13], mate).start()

    for n in (0, 1):
        for h in (0, 1):
            arrived(yi.at[n, half(h)], r_out.at[9 + 2 * n + h])
    finish(0, lambda r: ya[r, :] + yi[0, r, :].astype(F32) + yi[1, r, :].astype(F32))
    arrived(zr.at[0], r_out.at[4])
    for j in (0, 1):
        arrived(zi.at[j], r_out.at[7 + j])
    finish(1, lambda r: zm[0, r, :] + zr[0, r, :] + zi[0, r, :].astype(F32) + zi[1, r, :].astype(F32))
    arrived(out_ref.at[0, other_rows], r_out.at[13])
    rcopy(ends.at[0], ends.at[0], s_out.at[13], r_out.at[13], mate).wait_send()
    drain()


def on_device(embeddings, loss_weights, dataset_of_block, logit_scale):
    vmem = pl.BlockSpec(memory_space=pltpu.VMEM)
    smem = pl.BlockSpec(memory_space=pltpu.SMEM)
    dma = pltpu.SemaphoreType.DMA
    scratch = [
        pltpu.VMEM((UNITS, HALF, D), BF16),
        pltpu.VMEM((13, HALF, BLK), F32),
        pltpu.VMEM((13, HALF, BLK), BF16),
        pltpu.VMEM((2, 8, BLK), F32),
        pltpu.VMEM((5, HALF, 128), F32),
        pltpu.VMEM((5, HALF, 128), F32),
        pltpu.VMEM((3, 8, BLK), F32),
        pltpu.VMEM((3, 8, BLK), F32),
        pltpu.VMEM((5, 2, HALF), F32),
        pltpu.VMEM((5, 2, HALF), F32),
        pltpu.VMEM((5, 1, HALF), F32),
        pltpu.VMEM((5, HALF, 128), F32),
        pltpu.VMEM((3, 2, BLK), F32),
        pltpu.VMEM((5, 2, BLK), F32),
        pltpu.VMEM((3, 1, BLK), F32),
        pltpu.VMEM((HALF, D), F32),
        pltpu.VMEM((2, HALF, D), F32),
        pltpu.VMEM((2, HALF, D), BF16),
        pltpu.VMEM((2, HALF, D), BF16),
        pltpu.VMEM((HALF, D), BF16),
        pltpu.VMEM((2, QUART, D), BF16),
        pltpu.VMEM((HALF, D), BF16),
        pltpu.VMEM((HALF, D), BF16),
        pltpu.VMEM((3, HALF, D), F32),
        pltpu.VMEM((3, HALF, D), F32),
        pltpu.VMEM((3, HALF, D), F32),
        pltpu.VMEM((2, HALF, D), BF16),
        pltpu.VMEM((2, HALF, D), BF16),
        pltpu.VMEM((2, HALF, D), F32),
        dma((11,)), dma((1,)), dma((5,)), dma((UNITS, 2)), dma((15,)), dma((15,)), dma((14,)), dma((14,)),
    ]
    return pl.pallas_call(
        kernel,
        out_shape=jax.ShapeDtypeStruct((1, BLK, D), F32),
        in_specs=[smem, smem, vmem, vmem],
        out_specs=vmem,
        scratch_shapes=scratch,
        compiler_params=pltpu.CompilerParams(
            collective_id=0, has_side_effects=True, vmem_limit_bytes=56 * 2**20),
    )(dataset_of_block, logit_scale, embeddings, loss_weights)


def solution(mesh):
    in_specs = (P("tower", "tile", None), P("tower", "tile"), P(), P())
    return jax.shard_map(
        on_device, mesh=mesh, in_specs=in_specs, out_specs=P("tower", "tile", None), check_vma=False)
```

```python
import jax
import jax.numpy as jnp
from jax import lax
from jax.experimental import pallas as pl
from jax.experimental.pallas import tpu as pltpu
from jax.sharding import PartitionSpec as P


MESH = pl.DeviceIdType.MESH
F32, BF16 = jnp.float32, jnp.bfloat16
BLK, D = 512, 1024
HALF, PART = BLK // 2, BLK // 8
COLS, LINES = 4, 32
NEG = -1e30
LOG2E = 1.4426950408889634
CH = 64

UNITS = 11


def kernel(ds_ref, scale_ref, x_ref, wt_ref, out_ref, held, score, mass, wts,
           row_m, row_l, col_m, col_l, lp, li, lf, lcol, mp, mi, mf,
           ya, yp, yo, yi, yt, yr, xs, xo, zf, zr, zo, zi, ends,
           s_in, r_in, s_held, r_held, s_mid, r_mid, s_out, r_out, s_y, r_y, s_z, r_z, s_home, s_away, r_away):
    t = lax.axis_index("tower")
    tile = lax.axis_index("tile")
    line, y = tile // COLS, tile % COLS
    sel = y // 2
    sgn = 1 - 2 * sel
    edge = y % 3 == 0
    edge_k = 3 - 2 * sel
    edge_u = 2 - sel
    edge_b = 2 - sel
    late_b = 1 + sel

    def at(core, down, right):
        return (core, ((line + down + LINES) % LINES) * COLS + (y + right) % COLS)

    def rcopy(src, dst, ss, rs, dev):
        return pltpu.make_async_remote_copy(
            src_ref=src, dst_ref=dst, send_sem=ss, recv_sem=rs, device_id=dev, device_id_type=MESH)

    mate = at(1 - t, 0, 0)
    across = at(t, -sgn, edge_k)

    def arrived(ref, sem):
        rcopy(ref, ref, sem, sem, mate).wait_recv()

    barrier = pltpu.get_barrier_semaphore()
    peers = [mate, at(t, 0, 2)]
    for core in (0, 1):
        for k in (1, 3):
            peers.append(at(core, 0, k))
        for dz in (1, -1):
            peers.append(at(core, dz, 0))
    for dev in peers:
        pl.semaphore_signal(barrier, inc=1, device_id=dev, device_id_type=MESH)

    @pl.when(edge)
    def _():
        pl.semaphore_signal(barrier, inc=1, device_id=across, device_id_type=MESH)

    waiting = []
    for g in (0, 1):
        own = (1 - t) * (10 * g) + t * (4 + g)
        waiting.append(pltpu.make_async_copy(x_ref.at[0, pl.ds(HALF * g, HALF)], held.at[own], s_in.at[19 + g]))
        waiting[-1].start()
    wts[t] = jnp.broadcast_to(wt_ref[...].astype(F32), (8, BLK))
    col_m[...] = jnp.full(col_m.shape, NEG, F32)
    col_l[...] = jnp.zeros(col_l.shape, F32)
    row_m[4] = jnp.full((HALF, 128), NEG, F32)
    row_l[4] = jnp.zeros((HALF, 128), F32)
    pl.semaphore_wait(barrier, len(peers) + edge.astype(jnp.int32))

    pending, edge_pending = [], []

    def go(copy):
        copy.start()
        pending.append(copy)

    def edge_go(copy):
        edge_pending.append(copy)

        @pl.when(edge)
        def _():
            copy.start()

    def drain():
        for copy in pending:
            copy.wait_send()
        for step in range(4):
            for way in (0, 1):
                @pl.when(jnp.logical_not(direct[4 * step + 2 * way][1]))
                def _():
                    for g in (0, 1):
                        direct[4 * step + 2 * way + g][0].wait_send()

        @pl.when(edge)
        def _():
            for copy in edge_pending:
                copy.wait_send()

    def half(h):
        return pl.ds(HALF // 2 * h, HALF // 2)

    def part(q):
        return pl.ds(PART * q if isinstance(q, int) else pl.multiple_of(PART * q, PART), PART)

    direct = []
    for step in range(4):
        for way in (0, 1):
            q = step if way == 0 else 3 - step
            held_back = edge & (sel == way) & (t == 1)
            for g in (0, 1):
                sign = 1 - 2 * way
                unit = (1 - t) * (2 - way) + t * (6 + 2 * way + g)
                copy = rcopy(x_ref.at[0, pl.ds(HALF * g + PART * q, PART)], held.at[unit, part(q)],
                             s_in.at[4 * step + 2 * way + g], r_held.at[unit, q], at(g, t * sign, (1 - t) * sign))
                direct.append((copy, held_back))

    for g in (0, 1):
        unit = (1 - t) * (10 - 10 * g) + t * (4 + g)
        go(rcopy(x_ref.at[0, pl.ds(HALF * g, HALF)], held.at[unit], s_in.at[16 + g], r_held.at[unit, 0], mate))
    go(rcopy(wts.at[t], wts.at[t], s_in.at[18], r_in.at[0], mate))
    for step in range(4):
        for way in (0, 1):
            @pl.when(jnp.logical_not(direct[4 * step + 2 * way][1]))
            def _():
                for g in (0, 1):
                    direct[4 * step + 2 * way + g][0].start()

    def block_of(down, right):
        return ds_ref[((line + down + LINES) % LINES) * COLS + (y + right) % COLS]

    def factors(mine, other):
        live = mine == other
        temper = scale_ref[mine] * LOG2E
        return jnp.where(live, temper, 0.0), jnp.where(live, 0.0, NEG)

    def video(b):
        return held[pl.ds(4 + 2 * b, 2)].reshape(BLK, D)

    def multiply(first, count, b, index):
        score[pl.ds(index, count)] = lax.dot_general(
            held[pl.ds(first, count)].reshape(count * HALF, D), video(b), (((1,), (1,)), ((), ())),
            preferred_element_type=F32).reshape(count, HALF, BLK)

    def fold(slot, blocks):
        def rows(c, tops):
            at_rows = pl.ds(pl.multiple_of(c * CH, CH), CH)
            parts, peaks = [], []
            for n, (b, index, mult, off) in enumerate(blocks):
                s = score[index, at_rows, :] * mult + off
                score[index, at_rows, :] = s
                peak = tops[n]
                for e in range(0, CH, 8):
                    peak = jnp.maximum(peak, s[e:e + 8])
                peaks.append(peak)
                parts.extend([s[:, 128 * q:128 * q + 128] for q in range(4)])
            top = parts[0]
            for part in parts[1:]:
                top = jnp.maximum(top, part)
            total = jnp.exp2(parts[0] - top)
            for part in parts[1:]:
                total = total + jnp.exp2(part - top)
            row_m[slot, at_rows, :] = top
            row_l[slot, at_rows, :] = total
            return tuple(peaks)

        old = [col_m[b] for b, _, _, _ in blocks]
        new = lax.fori_loop(0, HALF // CH, rows, tuple(old))

        def columns(c, sums):
            at_rows = pl.ds(pl.multiple_of(c * CH, CH), CH)
            result = []
            for n, (b, index, mult, off) in enumerate(blocks):
                s = score[index, at_rows, :]
                total = sums[n]
                for e in range(0, CH, 8):
                    total = total + jnp.exp2(s[e:e + 8] - new[n])
                result.append(total)
            return tuple(result)

        begin = tuple(col_l[b] * jnp.exp2(old[n] - new[n]) for n, (b, _, _, _) in enumerate(blocks))
        sums = lax.fori_loop(0, HALF // CH, columns, begin)
        for n, (b, _, _, _) in enumerate(blocks):
            col_m[b] = new[n]
            col_l[b] = sums[n]

    def tile_of(u, b):
        k = u ^ (u // 2)
        return (b, 4 * b + u) + factors(block_of(0, k), block_of((b == 2) * 1 - (b == 1) * 1, 0))

    for copy in waiting:
        copy.wait()
    for g in (0, 1):
        unit = t * (10 - 10 * g) + (1 - t) * (4 + g)
        arrived(held.at[unit], r_held.at[unit, 0])
    arrived(wts.at[1 - t], r_in.at[0])

    multiply(0, 1, 0, 0)
    fold(0, [tile_of(0, 0)])

    give = edge & (block_of(0, edge_k) == block_of(2 * sgn, 0))
    for step in range(4):
        for unit, q in ((2, step), (1, 3 - step)):
            arrived(held.at[unit, part(q)], r_held.at[unit, q])
        if step == 2:
            for unit, h, way in ((2, 0, 1), (1, 1, -1)):
                go(rcopy(held.at[unit, half(h)], held.at[3, half(h)], s_held.at[h], r_held.at[3, h], at(t, 0, way)))
        q = step + sel * (3 - 2 * step)

        @pl.when(edge)
        def _():
            xs[part(q)] = jnp.where(give, held[edge_u, part(q), :], held[4 + t, part(q), :])

        unit = 4 + 2 * late_b + t
        edge_go(rcopy(xs.at[part(q)], held.at[unit, part(q)], s_held.at[4 + step], r_held.at[unit, q], at(t, sgn, 0)))

    def share(b, sem):
        unit = 4 + 2 * b + t
        for step in range(4):
            q = step if sem < 12 else step + sel * (3 - 2 * step)
            arrived(held.at[unit, part(q)], r_held.at[unit, q])
            go(rcopy(held.at[unit, part(q)], held.at[unit, part(q)], s_held.at[sem + step], r_held.at[unit, q], mate))

    def shared(b):
        unit = 4 + 2 * b + 1 - t
        for q in range(4):
            arrived(held.at[unit, part(q)], r_held.at[unit, q])

    share(edge_b, 8)
    shared(edge_b)

    multiply(1, 2, 0, 1)
    multiply(0, 3, edge_b, 4 * edge_b)
    fold(5, [tile_of(0, edge_b)])

    def early(u, carry):
        fold(u, [tile_of(u, 0), tile_of(u, edge_b)])
        return carry

    lax.fori_loop(1, 3, early, 0)
    share(late_b, 12)

    lane = lax.broadcasted_iota(jnp.int32, (HALF, 128), 1)

    def unite(u, slot):
        m, other = row_m[u], row_m[slot]
        top = jnp.maximum(m, other)
        row_l[u] = row_l[u] * jnp.exp2(m - top) + row_l[slot] * jnp.exp2(other - top)
        row_m[u] = top

    def pack_rows(u):
        m, l = row_m[u], row_l[u]
        top = jnp.max(m, axis=1, keepdims=True)
        total = jnp.sum(l * jnp.exp2(m - top), axis=1, keepdims=True)
        lp[u] = jnp.where(lane == 0, top, total).T[0:2, :]

    def send_rows(u):
        k = u ^ (u // 2)
        go(rcopy(lp.at[u], li.at[k - 1], s_mid.at[4 + k], r_mid.at[4 + k], at(t, 0, k)))

    @pl.when(edge)
    def _():
        multiply(4 + 2 * late_b + t, 1, edge_b, 12)
        fold(4, [(edge_b, 12) + factors(block_of(-sgn, edge_k), block_of(sgn, 0))])
        pack_rows(4)

    edge_go(rcopy(lp.at[4], li.at[4], s_mid.at[8], r_mid.at[8], across))
    shared(late_b)
    multiply(0, 3, late_b, 4 * late_b)

    def late(u, carry):
        fold(6 + u, [tile_of(u, late_b)])
        return carry

    lax.fori_loop(0, 3, late, 0)

    for u, slot in ((1, 7), (2, 8)):
        unite(u, slot)
        pack_rows(u)
        send_rows(u)
    for h in (0, 1):
        arrived(held.at[3, half(h)], r_held.at[3, h])
    for b in (0, 1, 2):
        multiply(3, 1, b, 4 * b + 3)
    fold(3, [tile_of(3, b) for b in (0, 1, 2)])
    pack_rows(3)
    send_rows(3)
    sub = lax.broadcasted_iota(jnp.int32, (2, BLK), 0)

    def pack_columns(b, carry):
        m, l = col_m[b], col_l[b]
        top = jnp.max(m, axis=0, keepdims=True)
        total = jnp.sum(l * jnp.exp2(m - top), axis=0, keepdims=True)
        mp[b] = jnp.where(sub == 0, top, total)
        return carry

    lax.fori_loop(0, 3, pack_columns, 0)
    for j in (0, 1):
        for g in (0, 1):
            go(rcopy(mp.at[j + 1], mi.at[2 * j + t], s_mid.at[2 * j + g], r_mid.at[2 * j + t],
                     at(g, (-1, 1)[j], 0)))
    go(rcopy(mp.at[0], mi.at[4], s_mid.at[4], r_mid.at[4], mate))
    for slot in (5, 6):
        unite(0, slot)
    pack_rows(0)
    li[3] = jnp.where(sub[:, 0:HALF] == 0, NEG, 0.0)

    def merge(parts):
        tops = [p[0:1, :] for p in parts]
        top = tops[0]
        for other in tops[1:]:
            top = jnp.maximum(top, other)
        total = parts[0][1:2, :] * jnp.exp2(tops[0] - top)
        for n in range(1, len(parts)):
            total = total + parts[n][1:2, :] * jnp.exp2(tops[n] - top)
        return top + jnp.log(total) * LOG2E

    for n in range(5):
        arrived(mi.at[n], r_mid.at[n])
    mf[0] = merge([mp[0]] + [mi[n] for n in range(5)]) - jnp.log(wts[1][0:1, :]) * LOG2E
    for j in (0, 1):
        go(rcopy(mf.at[0], mf.at[j + 1], s_mid.at[9 + j], r_mid.at[9 + j], at(t, (1, -1)[j], 0)))
    for k in (1, 2, 3):
        arrived(li.at[k - 1], r_mid.at[4 + k])

    @pl.when(edge)
    def _():
        arrived(li.at[4], r_mid.at[8])
        li[3] = li[4]

    w_half = wts[0, :, pl.ds(pl.multiple_of(HALF * t, HALF), HALF)][0:1, :]
    lf[0] = merge([lp[0]] + [li[n] for n in range(4)]) - jnp.log(w_half) * LOG2E
    for k in (1, 2, 3):
        go(rcopy(lf.at[0], lf.at[(4 - k) ^ ((4 - k) // 2)], s_mid.at[10 + k], r_mid.at[10 + 4 - k], at(t, 0, k)))

    edge_go(rcopy(lf.at[0], lf.at[4], s_mid.at[14], r_mid.at[14], across))

    for k in (1, 2, 3):
        arrived(lf.at[k ^ (k // 2)], r_mid.at[10 + k])

    def turn(k):
        lcol[k] = jnp.broadcast_to(lf[k], (128, HALF)).T

    for k in range(4):
        turn(k)
    for j in (0, 1):
        arrived(mf.at[j + 1], r_mid.at[9 + j])

    def derive(slot, blocks, diagonal=False):
        cols = [jnp.broadcast_to(mf[b], (CH, BLK)) for b, _ in blocks]

        def rows(c, carry):
            at_rows = pl.ds(pl.multiple_of(c * CH, CH), CH)
            lse = jnp.concatenate([lcol[slot, at_rows, :]] * 4, axis=1)
            for n, (b, index) in enumerate(blocks):
                s = score[index, at_rows, :]
                g = jnp.exp2(s - lse) + jnp.exp2(s - cols[n])
                if diagonal:
                    r_id = lax.broadcasted_iota(jnp.int32, (CH, BLK), 0) + c * CH + HALF * t
                    c_id = lax.broadcasted_iota(jnp.int32, (CH, BLK), 1)
                    both = jnp.broadcast_to(wts[0][0:1, :] + wts[1][0:1, :], (CH, BLK))
                    g = g - jnp.where(r_id == c_id, both, 0.0)
                mass[index, at_rows, :] = g.astype(BF16)
            return carry

        lax.fori_loop(0, HALF // CH, rows, 0)

    def derive_units(first, last, blocks):
        def one(u, carry):
            derive(u, [(b, 4 * b + u) for b in blocks])
            return carry

        lax.fori_loop(first, last, one, 0)

    def row_grad(first, count):
        def term(b):
            return jnp.dot(mass[4 * b + first:4 * b + first + count].reshape(count * HALF, BLK), video(b),
                           preferred_element_type=F32)

        return term(0) + term(1) + term(2)

    mine = pl.ds(pl.multiple_of(HALF * t, HALF), HALF)
    others = pl.ds(pl.multiple_of(HALF * (1 - t), HALF), HALF)

    def col_grad(b, sem, far=False):
        for rows in (others, mine):
            g = mass[pl.ds(4 * b, 4), :, rows].reshape(4 * HALF, HALF)
            a = held[0:4].reshape(4 * HALF, D)
            zf[b, rows] = lax.dot_general(g, a, (((0,), (0,)), ((), ())), preferred_element_type=F32)
            if far:
                @pl.when(edge)
                def _():
                    zf[b, rows] += lax.dot_general(mass[12, :, rows], held[4 + 2 * late_b + t],
                                                   (((0,), (0,)), ((), ())), preferred_element_type=F32)
            if rows is others:
                go(rcopy(zf.at[b, others], zr.at[b], s_out.at[sem], r_out.at[sem], mate))

    @pl.when(edge)
    def _():
        arrived(lf.at[4], r_mid.at[14])
        turn(4)
        derive(4, [(edge_b, 12)])

    derive_units(0, 4, (late_b,))
    col_grad(late_b, 5)

    @pl.when(edge)
    def _():
        xo[...] = jnp.dot(mass[12], video(edge_b), preferred_element_type=F32)

    derive_units(3, 4, (0, edge_b))

    def send_lines(b, sem, base, down, order):
        arrived(zr.at[b], r_out.at[sem])
        zo[b - 1] = (zf[b, mine] + zr[b]).astype(BF16)
        for step in range(4):
            q = step + order * (3 - 2 * step)
            go(rcopy(zo.at[b - 1, part(q)], zi.at[b - 1, part(q)], s_z.at[base, q], r_z.at[b - 1, q],
                     at(t, down, 0)))

    @pl.when(edge)
    def _():
        zf[late_b, mine] += xo[...]

    send_lines(late_b, 5, 0, -sgn, sel)
    yt[...] = row_grad(3, 1).astype(BF16)
    for h, way in ((0, 1), (1, -1)):
        go(rcopy(yt.at[half(h)], yr.at[h], s_out.at[2 + h], r_out.at[2 + h], at(t, 0, way)))
    derive_units(0, 3, (edge_b,))
    col_grad(edge_b, 6, True)
    derive(0, [(0, 0)], True)
    derive_units(1, 3, (0,))
    yp[...] = row_grad(1, 2).reshape(2, HALF, D)
    send_lines(edge_b, 6, 1, sgn, 1 - sel)

    for step in range(4):
        q = step + sel * (3 - 2 * step)

        @pl.when(edge)
        def _():
            arrived(zi.at[sel, part(q)], r_z.at[sel, q])
            yp[1 - sel, part(q)] += jnp.where(give, zi[sel, part(q), :].astype(F32), 0.0)

        if step == 2:
            for n in (0, 1):
                arrived(yr.at[n], r_out.at[2 + n])
                yp[n, half(n)] += yr[n].astype(F32)
        for n, q in ((0, 3 - step), (1, step)):
            yo[n, part(q)] = yp[n, part(q)].astype(BF16)
            go(rcopy(yo.at[n, part(q)], yi.at[n, part(q)], s_y.at[n, q], r_y.at[n, q], at(t, 0, 1 - 2 * n)))

    col_grad(0, 4)
    ya[...] = row_grad(0, 1)

    temper = scale_ref[block_of(0, 0)]
    home, away = [], []
    for q in range(4):
        to = out_ref.at[0, pl.ds(pl.multiple_of(HALF * t + PART * q, PART), PART)]
        home.append(pltpu.make_async_copy(ends.at[t, part(q)], to, s_home.at[q]))
        away.append(rcopy(ends.at[1 - t, part(q)], to, s_away.at[q], r_away.at[q], mate))

    def finish(mode, q, value):
        ends[mode, part(q)] = temper * value

        @pl.when(t == mode)
        def _():
            home[q].start()

        @pl.when(t != mode)
        def _():
            away[q].start()

    arrived(zr.at[0], r_out.at[4])
    for q in (1, 2, 0, 3):
        rows = part(q)
        for n in (0, 1):
            arrived(yi.at[n, rows], r_y.at[n, q])
        finish(0, q, ya[rows, :] + yi[0, rows, :].astype(F32) + yi[1, rows, :].astype(F32))
        for j in (0, 1):
            @pl.when(jnp.logical_not(edge & (sel == j)))
            def _():
                arrived(zi.at[j, rows], r_z.at[j, q])

        mine_q = pl.ds(pl.multiple_of(HALF * t + PART * q, PART), PART)
        finish(1, q, (zf[0, mine_q, :] + zr[0, rows, :]
                      + jnp.where(give & (sel == 0), 0.0, zi[0, rows, :].astype(F32))
                      + jnp.where(give & (sel == 1), 0.0, zi[1, rows, :].astype(F32))))
    for q in range(4):
        home[q].wait()
        away[q].wait_send()
        to = out_ref.at[0, pl.ds(pl.multiple_of(HALF * (1 - t) + PART * q, PART), PART)]
        rcopy(to, to, s_away.at[q], r_away.at[q], mate).wait_recv()
    drain()


def on_device(embeddings, loss_weights, dataset_of_block, logit_scale):
    vmem = pl.BlockSpec(memory_space=pltpu.VMEM)
    smem = pl.BlockSpec(memory_space=pltpu.SMEM)
    hbm = pl.BlockSpec(memory_space=pl.ANY)
    dma = pltpu.SemaphoreType.DMA
    scratch = [
        pltpu.VMEM((UNITS, HALF, D), BF16),
        pltpu.VMEM((13, HALF, BLK), F32),
        pltpu.VMEM((13, HALF, BLK), BF16),
        pltpu.VMEM((2, 8, BLK), F32),
        pltpu.VMEM((9, HALF, 128), F32),
        pltpu.VMEM((9, HALF, 128), F32),
        pltpu.VMEM((3, 8, BLK), F32),
        pltpu.VMEM((3, 8, BLK), F32),
        pltpu.VMEM((5, 2, HALF), F32),
        pltpu.VMEM((5, 2, HALF), F32),
        pltpu.VMEM((5, 1, HALF), F32),
        pltpu.VMEM((5, HALF, 128), F32),
        pltpu.VMEM((3, 2, BLK), F32),
        pltpu.VMEM((5, 2, BLK), F32),
        pltpu.VMEM((3, 1, BLK), F32),
        pltpu.VMEM((HALF, D), F32),
        pltpu.VMEM((2, HALF, D), F32),
        pltpu.VMEM((2, HALF, D), BF16),
        pltpu.VMEM((2, HALF, D), BF16),
        pltpu.VMEM((HALF, D), BF16),
        pltpu.VMEM((2, HALF // 2, D), BF16),
        pltpu.VMEM((HALF, D), BF16),
        pltpu.VMEM((HALF, D), F32),
        pltpu.VMEM((3, BLK, D), F32),
        pltpu.VMEM((3, HALF, D), F32),
        pltpu.VMEM((2, HALF, D), BF16),
        pltpu.VMEM((2, HALF, D), BF16),
        pltpu.VMEM((2, HALF, D), F32),
        dma((21,)), dma((1,)), dma((16,)), dma((UNITS, 4)), dma((15,)), dma((15,)), dma((14,)), dma((14,)),
        dma((2, 4)), dma((2, 4)), dma((2, 4)), dma((2, 4)), dma((4,)), dma((4,)), dma((4,)),
    ]
    return pl.pallas_call(
        kernel,
        out_shape=jax.ShapeDtypeStruct((1, BLK, D), F32),
        in_specs=[smem, smem, hbm, vmem],
        out_specs=hbm,
        scratch_shapes=scratch,
        compiler_params=pltpu.CompilerParams(
            collective_id=0, has_side_effects=True, vmem_limit_bytes=56 * 2**20),
    )(dataset_of_block, logit_scale, embeddings, loss_weights)


def solution(mesh):
    in_specs = (P("tower", "tile", None), P("tower", "tile"), P(), P())
    return jax.shard_map(
        on_device, mesh=mesh, in_specs=in_specs, out_specs=P("tower", "tile", None), check_vma=False)
```

```python
import jax
import jax.numpy as jnp
from jax import lax
from jax.experimental import pallas as pl
from jax.experimental.pallas import tpu as pltpu
from jax.sharding import PartitionSpec as P


MESH = pl.DeviceIdType.MESH
F32, BF16 = jnp.float32, jnp.bfloat16
BLK, D = 512, 1024
HALF, PART = BLK // 2, BLK // 8
COLS, LINES = 4, 32
NEG = -1e30
LOG2E = 1.4426950408889634
CH = 64

UNITS = 11


def kernel(ds_ref, scale_ref, x_ref, wt_ref, out_ref, held, score, mass, wts,
           row_m, row_l, col_m, col_l, lp, li, lx, lf, lcol, mp, m1, m2, m3, mf,
           ya, yp, yo, yi, yt, yr, xs, xo, zf, zr, zo, zi, ends,
           s_in, r_in, s_held, r_held, s_mid, r_mid, s_out, r_out, s_y, r_y, s_z, r_z, s_home, s_away, r_away):
    t = lax.axis_index("tower")
    tile = lax.axis_index("tile")
    line, y = tile // COLS, tile % COLS
    sel = y // 2
    sgn = 1 - 2 * sel
    edge = y % 3 == 0
    edge_k = 3 - 2 * sel
    edge_u = 2 - sel
    edge_b = 2 - sel
    late_b = 1 + sel

    def at(core, down, right):
        return (core, ((line + down + LINES) % LINES) * COLS + (y + right) % COLS)

    def rcopy(src, dst, ss, rs, dev):
        return pltpu.make_async_remote_copy(
            src_ref=src, dst_ref=dst, send_sem=ss, recv_sem=rs, device_id=dev, device_id_type=MESH)

    mate = at(1 - t, 0, 0)
    across = at(t, -sgn, edge_k)

    def arrived(ref, sem):
        rcopy(ref, ref, sem, sem, mate).wait_recv()

    barrier = pltpu.get_barrier_semaphore()
    peers = [mate, at(t, 0, 2)]
    for core in (0, 1):
        for k in (1, 3):
            peers.append(at(core, 0, k))
        for dz in (1, -1, 2, -2):
            peers.append(at(core, dz, 0))
    peers.append(at(t, 1, COLS - y))
    peers.append(at(t, -1, COLS - 1 - y))
    for dev in peers:
        pl.semaphore_signal(barrier, inc=1, device_id=dev, device_id_type=MESH)

    @pl.when(edge)
    def _():
        for c in range(COLS):
            pl.semaphore_signal(barrier, inc=1, device_id=at(t, -sgn, c), device_id_type=MESH)

    waiting = []
    for g in (0, 1):
        own = (1 - t) * (10 * g) + t * (4 + g)
        waiting.append(pltpu.make_async_copy(x_ref.at[0, pl.ds(HALF * g, HALF)], held.at[own], s_in.at[19 + g]))
        waiting[-1].start()
    wts[t] = jnp.broadcast_to(wt_ref[...].astype(F32), (8, BLK))
    col_m[...] = jnp.full(col_m.shape, NEG, F32)
    col_l[...] = jnp.zeros(col_l.shape, F32)
    row_m[4] = jnp.full((HALF, 128), NEG, F32)
    row_l[4] = jnp.zeros((HALF, 128), F32)
    pl.semaphore_wait(barrier, len(peers) + COLS * edge.astype(jnp.int32))

    pending, edge_pending = [], []

    def go(copy):
        copy.start()
        pending.append(copy)

    def edge_go(copy):
        edge_pending.append(copy)

        @pl.when(edge)
        def _():
            copy.start()

    def drain():
        for copy in pending:
            copy.wait_send()
        for step in range(4):
            for way in (0, 1):
                @pl.when(jnp.logical_not(direct[4 * step + 2 * way][1]))
                def _():
                    for g in (0, 1):
                        direct[4 * step + 2 * way + g][0].wait_send()

        @pl.when(edge)
        def _():
            for copy in edge_pending:
                copy.wait_send()

    def half(h):
        return pl.ds(HALF // 2 * h, HALF // 2)

    def part(q):
        return pl.ds(PART * q if isinstance(q, int) else pl.multiple_of(PART * q, PART), PART)

    direct = []
    for step in range(4):
        for way in (0, 1):
            q = step if way == 0 else 3 - step
            held_back = edge & (sel == way) & (t == 1)
            for g in (0, 1):
                sign = 1 - 2 * way
                unit = (1 - t) * (2 - way) + t * (6 + 2 * way + g)
                copy = rcopy(x_ref.at[0, pl.ds(HALF * g + PART * q, PART)], held.at[unit, part(q)],
                             s_in.at[4 * step + 2 * way + g], r_held.at[unit, q], at(g, t * sign, (1 - t) * sign))
                direct.append((copy, held_back))

    for g in (0, 1):
        unit = (1 - t) * (10 - 10 * g) + t * (4 + g)
        go(rcopy(x_ref.at[0, pl.ds(HALF * g, HALF)], held.at[unit], s_in.at[16 + g], r_held.at[unit, 0], mate))
    go(rcopy(wts.at[t], wts.at[t], s_in.at[18], r_in.at[0], mate))
    for step in range(4):
        for way in (0, 1):
            @pl.when(jnp.logical_not(direct[4 * step + 2 * way][1]))
            def _():
                for g in (0, 1):
                    direct[4 * step + 2 * way + g][0].start()

    def block_of(down, right):
        return ds_ref[((line + down + LINES) % LINES) * COLS + (y + right) % COLS]

    def factors(mine, other):
        live = mine == other
        temper = scale_ref[mine] * LOG2E
        return jnp.where(live, temper, 0.0), jnp.where(live, 0.0, NEG)

    def video(b):
        return held[pl.ds(4 + 2 * b, 2)].reshape(BLK, D)

    def multiply(first, count, b, index):
        score[pl.ds(index, count)] = lax.dot_general(
            held[pl.ds(first, count)].reshape(count * HALF, D), video(b), (((1,), (1,)), ((), ())),
            preferred_element_type=F32).reshape(count, HALF, BLK)

    def fold(slot, blocks):
        def rows(c, tops):
            at_rows = pl.ds(pl.multiple_of(c * CH, CH), CH)
            parts, peaks = [], []
            for n, (b, index, mult, off) in enumerate(blocks):
                s = score[index, at_rows, :] * mult + off
                score[index, at_rows, :] = s
                peak = tops[n]
                for e in range(0, CH, 8):
                    peak = jnp.maximum(peak, s[e:e + 8])
                peaks.append(peak)
                parts.extend([s[:, 128 * q:128 * q + 128] for q in range(4)])
            top = parts[0]
            for part in parts[1:]:
                top = jnp.maximum(top, part)
            total = jnp.exp2(parts[0] - top)
            for part in parts[1:]:
                total = total + jnp.exp2(part - top)
            row_m[slot, at_rows, :] = top
            row_l[slot, at_rows, :] = total
            return tuple(peaks)

        old = [col_m[b] for b, _, _, _ in blocks]
        new = lax.fori_loop(0, HALF // CH, rows, tuple(old))

        def columns(c, sums):
            at_rows = pl.ds(pl.multiple_of(c * CH, CH), CH)
            result = []
            for n, (b, index, mult, off) in enumerate(blocks):
                s = score[index, at_rows, :]
                total = sums[n]
                for e in range(0, CH, 8):
                    total = total + jnp.exp2(s[e:e + 8] - new[n])
                result.append(total)
            return tuple(result)

        begin = tuple(col_l[b] * jnp.exp2(old[n] - new[n]) for n, (b, _, _, _) in enumerate(blocks))
        sums = lax.fori_loop(0, HALF // CH, columns, begin)
        for n, (b, _, _, _) in enumerate(blocks):
            col_m[b] = new[n]
            col_l[b] = sums[n]

    def tile_of(u, b):
        k = u ^ (u // 2)
        return (b, 4 * b + u) + factors(block_of(0, k), block_of((b == 2) * 1 - (b == 1) * 1, 0))

    for copy in waiting:
        copy.wait()
    for g in (0, 1):
        unit = t * (10 - 10 * g) + (1 - t) * (4 + g)
        arrived(held.at[unit], r_held.at[unit, 0])
    arrived(wts.at[1 - t], r_in.at[0])
    log_w = jnp.log(wts[0, :, pl.ds(pl.multiple_of(HALF * t, HALF), HALF)][0:1, :]) * LOG2E
    lp[2, 0:1, :] = log_w
    mp[1, 2:3, :] = jnp.log(wts[1][0:1, :]) * LOG2E

    multiply(0, 1, 0, 0)
    fold(0, [tile_of(0, 0)])

    give = edge & (block_of(0, edge_k) == block_of(2 * sgn, 0))
    for step in range(4):
        for unit, q in ((2, step), (1, 3 - step)):
            arrived(held.at[unit, part(q)], r_held.at[unit, q])
        if step == 2:
            for unit, h, way in ((2, 0, 1), (1, 1, -1)):
                go(rcopy(held.at[unit, half(h)], held.at[3, half(h)], s_held.at[h], r_held.at[3, h], at(t, 0, way)))
        q = step + sel * (3 - 2 * step)

        @pl.when(edge)
        def _():
            xs[part(q)] = jnp.where(give, held[edge_u, part(q), :], held[4 + t, part(q), :])

        unit = 4 + 2 * late_b + t
        edge_go(rcopy(xs.at[part(q)], held.at[unit, part(q)], s_held.at[4 + step], r_held.at[unit, q], at(t, sgn, 0)))

    def share(b, sem):
        unit = 4 + 2 * b + t
        for step in range(4):
            q = step if sem < 12 else step + sel * (3 - 2 * step)
            arrived(held.at[unit, part(q)], r_held.at[unit, q])
            go(rcopy(held.at[unit, part(q)], held.at[unit, part(q)], s_held.at[sem + step], r_held.at[unit, q], mate))

    def shared(b):
        unit = 4 + 2 * b + 1 - t
        for q in range(4):
            arrived(held.at[unit, part(q)], r_held.at[unit, q])

    share(edge_b, 8)
    shared(edge_b)

    multiply(1, 2, 0, 1)
    multiply(0, 3, edge_b, 4 * edge_b)
    fold(5, [tile_of(0, edge_b)])

    def early(u, carry):
        fold(u, [tile_of(u, 0), tile_of(u, edge_b)])
        return carry

    lax.fori_loop(1, 3, early, 0)
    share(late_b, 12)

    lane = lax.broadcasted_iota(jnp.int32, (HALF, 128), 1)

    def unite(u, slot):
        m, other = row_m[u], row_m[slot]
        top = jnp.maximum(m, other)
        row_l[u] = row_l[u] * jnp.exp2(m - top) + row_l[slot] * jnp.exp2(other - top)
        row_m[u] = top

    def pack_rows(u):
        m, l = row_m[u], row_l[u]
        top = jnp.max(m, axis=1, keepdims=True)
        total = jnp.sum(l * jnp.exp2(m - top), axis=1, keepdims=True)
        turned = jnp.where(lane == 0, top, total).T
        if u == 4:
            lp[3, 0:2, :] = turned[0:2, :]
        else:
            lp[0, u:u + 1, :] = turned[0:1, :]
            lp[1, u:u + 1, :] = turned[1:2, :]

    @pl.when(edge)
    def _():
        multiply(4 + 2 * late_b + t, 1, edge_b, 12)
        fold(4, [(edge_b, 12) + factors(block_of(-sgn, edge_k), block_of(sgn, 0))])
        pack_rows(4)

    for c in range(COLS):
        edge_go(rcopy(lp.at[3], lx.at[sel], s_mid.at[c], r_mid.at[sel], at(t, -sgn, c)))
    shared(late_b)
    multiply(0, 3, late_b, 4 * late_b)

    def late(u, carry):
        fold(6 + u, [tile_of(u, late_b)])
        return carry

    lax.fori_loop(0, 3, late, 0)

    for u, slot in ((1, 7), (2, 8), (0, 5), (0, 6)):
        unite(u, slot)
    for u in (0, 1, 2):
        pack_rows(u)
    for h in (0, 1):
        arrived(held.at[3, half(h)], r_held.at[3, h])
    for b in (0, 1, 2):
        multiply(3, 1, b, 4 * b + 3)
    fold(3, [tile_of(3, b) for b in (0, 1, 2)])
    for n, b in ((0, 1), (1, 0), (2, 2)):
        m, l = col_m[b], col_l[b]
        top = jnp.max(m, axis=0, keepdims=True)
        mp[n, 0:1, :] = top
        mp[n, 1:2, :] = jnp.sum(l * jnp.exp2(m - top), axis=0, keepdims=True)
    for way in (0, 1):
        for g in (0, 1):
            go(rcopy(mp.at[way:way + 2], m1.at[way, t], s_mid.at[4 + 2 * way + g], r_mid.at[2 + 2 * way + t],
                     at(g, 2 * way - 1, 0)))
            go(rcopy(mp.at[2 * way], m2.at[way, t], s_mid.at[8 + 2 * way + g], r_mid.at[6 + 2 * way + t],
                     at(g, 4 * way - 2, 0)))
    go(rcopy(mp, m3, s_mid.at[12], r_mid.at[10], mate))
    pack_rows(3)
    for k in (2, 1, 3):
        go(rcopy(lp.at[0:3], li.at[k - 1], s_mid.at[12 + k], r_mid.at[10 + k], at(t, 0, k)))

    def merge(parts):
        tops = [m for m, _ in parts]
        top = tops[0]
        for other in tops[1:]:
            top = jnp.maximum(top, other)
        total = parts[0][1] * jnp.exp2(tops[0] - top)
        for n in range(1, len(parts)):
            total = total + parts[n][1] * jnp.exp2(tops[n] - top)
        return top + jnp.log(total) * LOG2E

    for way in (0, 1):
        arrived(lx.at[way], r_mid.at[way])
        for g in (0, 1):
            arrived(m1.at[way, g], r_mid.at[2 + 2 * way + g])
            arrived(m2.at[way, g], r_mid.at[6 + 2 * way + g])
    arrived(m3, r_mid.at[10])

    def pair(ref, *index):
        return ref[index + (slice(0, 1),)], ref[index + (slice(1, 2),)]

    both = (0, 1)
    mf[0] = merge([pair(mp, 1), pair(m3, 1)] + [pair(m1, 0, g, 0) for g in both] + [pair(m1, 1, g, 1) for g in both]
                  ) - mp[1, 2:3, :]
    mf[1] = merge([pair(mp, 0), pair(m3, 0)] + [pair(m1, 1, g, 0) for g in both] + [pair(m2, 1, g) for g in both]
                  ) - m1[1, 0, 0, 2:3, :]
    mf[2] = merge([pair(mp, 2), pair(m3, 2)] + [pair(m1, 0, g, 1) for g in both] + [pair(m2, 0, g) for g in both]
                  ) - m1[0, 0, 1, 2:3, :]
    for k in (1, 2, 3):
        arrived(li.at[k - 1], r_mid.at[10 + k])

    def line_of(ref, n):
        return ref[0, n:n + 1, :], ref[1, n:n + 1, :]

    def far_part(column):
        m = jnp.where(column == 3, lx[0, 0:1, :], jnp.where(column == 0, lx[1, 0:1, :], NEG))
        l = jnp.where(column == 3, lx[0, 1:2, :], jnp.where(column == 0, lx[1, 1:2, :], 0.0))
        return m, l

    for u in range(4):
        k = u ^ (u // 2)
        parts = [line_of(lp, u), far_part((y + k) % COLS)]
        for other in (1, 2, 3):
            theirs = (k - other) % 4
            parts.append(line_of(li.at[3 - other], theirs ^ (theirs // 2)))
        lf[u] = merge(parts) - (lp[2, 0:1, :] if k == 0 else li[3 - k, 2, 0:1, :])
    edge_go(rcopy(lf.at[0], lf.at[4], s_mid.at[16], r_mid.at[14], across))

    def turn(u):
        lcol[u] = jnp.broadcast_to(lf[u], (128, HALF)).T

    for u in range(4):
        turn(u)

    def derive(slot, blocks, diagonal=False):
        cols = [jnp.broadcast_to(mf[b], (CH, BLK)) for b, _ in blocks]

        def rows(c, carry):
            at_rows = pl.ds(pl.multiple_of(c * CH, CH), CH)
            lse = jnp.concatenate([lcol[slot, at_rows, :]] * 4, axis=1)
            for n, (b, index) in enumerate(blocks):
                s = score[index, at_rows, :]
                g = jnp.exp2(s - lse) + jnp.exp2(s - cols[n])
                if diagonal:
                    r_id = lax.broadcasted_iota(jnp.int32, (CH, BLK), 0) + c * CH + HALF * t
                    c_id = lax.broadcasted_iota(jnp.int32, (CH, BLK), 1)
                    both = jnp.broadcast_to(wts[0][0:1, :] + wts[1][0:1, :], (CH, BLK))
                    g = g - jnp.where(r_id == c_id, both, 0.0)
                mass[index, at_rows, :] = g.astype(BF16)
            return carry

        lax.fori_loop(0, HALF // CH, rows, 0)

    def derive_units(first, last, blocks):
        def one(u, carry):
            derive(u, [(b, 4 * b + u) for b in blocks])
            return carry

        lax.fori_loop(first, last, one, 0)

    def row_grad(first, count):
        def term(b):
            return jnp.dot(mass[4 * b + first:4 * b + first + count].reshape(count * HALF, BLK), video(b),
                           preferred_element_type=F32)

        return term(0) + term(1) + term(2)

    mine = pl.ds(pl.multiple_of(HALF * t, HALF), HALF)
    others = pl.ds(pl.multiple_of(HALF * (1 - t), HALF), HALF)

    def col_grad(b, sem, far=False):
        for rows in (others, mine):
            g = mass[pl.ds(4 * b, 4), :, rows].reshape(4 * HALF, HALF)
            a = held[0:4].reshape(4 * HALF, D)
            zf[b, rows] = lax.dot_general(g, a, (((0,), (0,)), ((), ())), preferred_element_type=F32)
            if far:
                @pl.when(edge)
                def _():
                    zf[b, rows] += lax.dot_general(mass[12, :, rows], held[4 + 2 * late_b + t],
                                                   (((0,), (0,)), ((), ())), preferred_element_type=F32)
            if rows is others:
                go(rcopy(zf.at[b, others], zr.at[b], s_out.at[sem], r_out.at[sem], mate))

    derive_units(0, 4, (late_b,))
    col_grad(late_b, 5)
    derive_units(3, 4, (0, edge_b))

    @pl.when(edge)
    def _():
        arrived(lf.at[4], r_mid.at[14])
        turn(4)
        derive(4, [(edge_b, 12)])
        xo[...] = jnp.dot(mass[12], video(edge_b), preferred_element_type=F32)

    def send_lines(b, sem, base, down, order):
        arrived(zr.at[b], r_out.at[sem])
        zo[b - 1] = (zf[b, mine] + zr[b]).astype(BF16)
        for step in range(4):
            q = step + order * (3 - 2 * step)
            go(rcopy(zo.at[b - 1, part(q)], zi.at[b - 1, part(q)], s_z.at[base, q], r_z.at[b - 1, q],
                     at(t, down, 0)))

    @pl.when(edge)
    def _():
        zf[late_b, mine] += xo[...]

    send_lines(late_b, 5, 0, -sgn, sel)
    yt[...] = row_grad(3, 1).astype(BF16)
    for h, way in ((0, 1), (1, -1)):
        go(rcopy(yt.at[half(h)], yr.at[h], s_out.at[2 + h], r_out.at[2 + h], at(t, 0, way)))
    derive_units(0, 3, (edge_b,))
    col_grad(edge_b, 6, True)
    derive(0, [(0, 0)], True)
    derive_units(1, 3, (0,))
    send_lines(edge_b, 6, 1, sgn, 1 - sel)
    yp[...] = row_grad(1, 2).reshape(2, HALF, D)

    for step in range(4):
        q = step + sel * (3 - 2 * step)

        @pl.when(edge)
        def _():
            arrived(zi.at[sel, part(q)], r_z.at[sel, q])
            yp[1 - sel, part(q)] += jnp.where(give, zi[sel, part(q), :].astype(F32), 0.0)

        if step == 2:
            for n in (0, 1):
                arrived(yr.at[n], r_out.at[2 + n])
                yp[n, half(n)] += yr[n].astype(F32)
        for n, q in ((0, 3 - step), (1, step)):
            yo[n, part(q)] = yp[n, part(q)].astype(BF16)
            go(rcopy(yo.at[n, part(q)], yi.at[n, part(q)], s_y.at[n, q], r_y.at[n, q], at(t, 0, 1 - 2 * n)))

    col_grad(0, 4)
    ya[...] = row_grad(0, 1)

    temper = scale_ref[block_of(0, 0)]
    home, away = [], []
    for q in range(4):
        to = out_ref.at[0, pl.ds(pl.multiple_of(HALF * t + PART * q, PART), PART)]
        home.append(pltpu.make_async_copy(ends.at[t, part(q)], to, s_home.at[q]))
        away.append(rcopy(ends.at[1 - t, part(q)], to, s_away.at[q], r_away.at[q], mate))

    def finish(mode, q, value):
        ends[mode, part(q)] = temper * value

        @pl.when(t == mode)
        def _():
            home[q].start()

        @pl.when(t != mode)
        def _():
            away[q].start()

    arrived(zr.at[0], r_out.at[4])
    for q in (1, 2, 0, 3):
        rows = part(q)
        for n in (0, 1):
            arrived(yi.at[n, rows], r_y.at[n, q])
        finish(0, q, ya[rows, :] + yi[0, rows, :].astype(F32) + yi[1, rows, :].astype(F32))
        for j in (0, 1):
            @pl.when(jnp.logical_not(edge & (sel == j)))
            def _():
                arrived(zi.at[j, rows], r_z.at[j, q])

        mine_q = pl.ds(pl.multiple_of(HALF * t + PART * q, PART), PART)
        finish(1, q, (zf[0, mine_q, :] + zr[0, rows, :]
                      + jnp.where(give & (sel == 0), 0.0, zi[0, rows, :].astype(F32))
                      + jnp.where(give & (sel == 1), 0.0, zi[1, rows, :].astype(F32))))
    for q in range(4):
        home[q].wait()
        away[q].wait_send()
        to = out_ref.at[0, pl.ds(pl.multiple_of(HALF * (1 - t) + PART * q, PART), PART)]
        rcopy(to, to, s_away.at[q], r_away.at[q], mate).wait_recv()
    drain()


def on_device(embeddings, loss_weights, dataset_of_block, logit_scale):
    vmem = pl.BlockSpec(memory_space=pltpu.VMEM)
    smem = pl.BlockSpec(memory_space=pltpu.SMEM)
    hbm = pl.BlockSpec(memory_space=pl.ANY)
    dma = pltpu.SemaphoreType.DMA
    scratch = [
        pltpu.VMEM((UNITS, HALF, D), BF16),
        pltpu.VMEM((13, HALF, BLK), F32),
        pltpu.VMEM((13, HALF, BLK), BF16),
        pltpu.VMEM((2, 8, BLK), F32),
        pltpu.VMEM((9, HALF, 128), F32),
        pltpu.VMEM((9, HALF, 128), F32),
        pltpu.VMEM((3, 8, BLK), F32),
        pltpu.VMEM((3, 8, BLK), F32),
        pltpu.VMEM((4, 4, HALF), F32),
        pltpu.VMEM((3, 3, 4, HALF), F32),
        pltpu.VMEM((2, 4, HALF), F32),
        pltpu.VMEM((5, 1, HALF), F32),
        pltpu.VMEM((5, HALF, 128), F32),
        pltpu.VMEM((3, 4, BLK), F32),
        pltpu.VMEM((2, 2, 2, 4, BLK), F32),
        pltpu.VMEM((2, 2, 4, BLK), F32),
        pltpu.VMEM((3, 4, BLK), F32),
        pltpu.VMEM((3, 1, BLK), F32),
        pltpu.VMEM((HALF, D), F32),
        pltpu.VMEM((2, HALF, D), F32),
        pltpu.VMEM((2, HALF, D), BF16),
        pltpu.VMEM((2, HALF, D), BF16),
        pltpu.VMEM((HALF, D), BF16),
        pltpu.VMEM((2, HALF // 2, D), BF16),
        pltpu.VMEM((HALF, D), BF16),
        pltpu.VMEM((HALF, D), F32),
        pltpu.VMEM((3, BLK, D), F32),
        pltpu.VMEM((3, HALF, D), F32),
        pltpu.VMEM((2, HALF, D), BF16),
        pltpu.VMEM((2, HALF, D), BF16),
        pltpu.VMEM((2, HALF, D), F32),
        dma((21,)), dma((1,)), dma((16,)), dma((UNITS, 4)), dma((17,)), dma((15,)), dma((14,)), dma((14,)),
        dma((2, 4)), dma((2, 4)), dma((2, 4)), dma((2, 4)), dma((4,)), dma((4,)), dma((4,)),
    ]
    return pl.pallas_call(
        kernel,
        out_shape=jax.ShapeDtypeStruct((1, BLK, D), F32),
        in_specs=[smem, smem, hbm, vmem],
        out_specs=hbm,
        scratch_shapes=scratch,
        compiler_params=pltpu.CompilerParams(
            collective_id=0, has_side_effects=True, vmem_limit_bytes=56 * 2**20),
    )(dataset_of_block, logit_scale, embeddings, loss_weights)


def solution(mesh):
    in_specs = (P("tower", "tile", None), P("tower", "tile"), P(), P())
    return jax.shard_map(
        on_device, mesh=mesh, in_specs=in_specs, out_specs=P("tower", "tile", None), check_vma=False)
```

```python
import jax
import jax.numpy as jnp
from jax import lax
from jax.experimental import pallas as pl
from jax.experimental.pallas import tpu as pltpu
from jax.sharding import PartitionSpec as P


MESH = pl.DeviceIdType.MESH
F32, BF16 = jnp.float32, jnp.bfloat16
BLK, D = 512, 1024
HALF, PART = BLK // 2, BLK // 8
COLS, LINES = 4, 32
NEG = -1e30
LOG2E = 1.4426950408889634
CH = 64

UNITS = 11


def kernel(ds_ref, scale_ref, x_ref, wt_ref, out_ref, held, score, mass, wts,
           row_m, row_l, col_m, col_l, lp, li, lx, lq, lf, lcol, mp, m1, m2, m3, mf,
           ya, yp, yo, yi, yt, yr, xs, zf, zr, zo, zi, ends,
           s_in, r_in, s_held, r_held, s_mid, r_mid, s_out, r_out, s_y, r_y, s_z, r_z, s_home, s_away, r_away):
    t = lax.axis_index("tower")
    tile = lax.axis_index("tile")
    line, y = tile // COLS, tile % COLS
    sel = y // 2
    sgn = 1 - 2 * sel
    edge = y % 3 == 0
    edge_k = 3 - 2 * sel
    edge_u = 2 - sel
    edge_b = 2 - sel
    late_b = 1 + sel

    def at(core, down, right):
        return (core, ((line + down + LINES) % LINES) * COLS + (y + right) % COLS)

    def rcopy(src, dst, ss, rs, dev):
        return pltpu.make_async_remote_copy(
            src_ref=src, dst_ref=dst, send_sem=ss, recv_sem=rs, device_id=dev, device_id_type=MESH)

    mate = at(1 - t, 0, 0)

    def arrived(ref, sem):
        rcopy(ref, ref, sem, sem, mate).wait_recv()

    barrier = pltpu.get_barrier_semaphore()
    peers = [mate, at(t, 0, 2)]
    for core in (0, 1):
        for k in (1, 3):
            peers.append(at(core, 0, k))
        for dz in (1, -1, 2, -2):
            peers.append(at(core, dz, 0))
    peers.append(at(t, 1, COLS - y))
    peers.append(at(t, -1, COLS - 1 - y))
    for dev in peers:
        pl.semaphore_signal(barrier, inc=1, device_id=dev, device_id_type=MESH)

    @pl.when(edge)
    def _():
        for c in range(COLS):
            pl.semaphore_signal(barrier, inc=1, device_id=at(t, -sgn, c), device_id_type=MESH)

    waiting = []
    for g in (0, 1):
        own = (1 - t) * (10 * g) + t * (4 + g)
        waiting.append(pltpu.make_async_copy(x_ref.at[0, pl.ds(HALF * g, HALF)], held.at[own], s_in.at[19 + g]))
        waiting[-1].start()
    wts[t] = jnp.broadcast_to(wt_ref[...].astype(F32), (8, BLK))
    col_m[...] = jnp.full(col_m.shape, NEG, F32)
    col_l[...] = jnp.zeros(col_l.shape, F32)
    row_m[4] = jnp.full((HALF, 128), NEG, F32)
    row_l[4] = jnp.zeros((HALF, 128), F32)
    pl.semaphore_wait(barrier, len(peers) + COLS * edge.astype(jnp.int32))

    pending, edge_pending = [], []

    def go(copy):
        copy.start()
        pending.append(copy)

    def edge_go(copy):
        edge_pending.append(copy)

        @pl.when(edge)
        def _():
            copy.start()

    def drain():
        for copy in pending:
            copy.wait_send()
        for step in range(4):
            for way in (0, 1):
                @pl.when(jnp.logical_not(direct[4 * step + 2 * way][1]))
                def _():
                    for g in (0, 1):
                        direct[4 * step + 2 * way + g][0].wait_send()

        @pl.when(edge)
        def _():
            for copy in edge_pending:
                copy.wait_send()

    def half(h):
        return pl.ds(HALF // 2 * h, HALF // 2)

    def part(q):
        return pl.ds(PART * q if isinstance(q, int) else pl.multiple_of(PART * q, PART), PART)

    direct = []
    for step in range(4):
        for way in (0, 1):
            q = step if way == 0 else 3 - step
            held_back = edge & (sel == way) & (t == 1)
            for g in (0, 1):
                sign = 1 - 2 * way
                unit = (1 - t) * (2 - way) + t * (6 + 2 * way + g)
                copy = rcopy(x_ref.at[0, pl.ds(HALF * g + PART * q, PART)], held.at[unit, part(q)],
                             s_in.at[4 * step + 2 * way + g], r_held.at[unit, q], at(g, t * sign, (1 - t) * sign))
                direct.append((copy, held_back))

    for g in (0, 1):
        unit = (1 - t) * (10 - 10 * g) + t * (4 + g)
        go(rcopy(x_ref.at[0, pl.ds(HALF * g, HALF)], held.at[unit], s_in.at[16 + g], r_held.at[unit, 0], mate))
    go(rcopy(wts.at[t], wts.at[t], s_in.at[18], r_in.at[0], mate))
    for step in range(4):
        for way in (0, 1):
            @pl.when(jnp.logical_not(direct[4 * step + 2 * way][1]))
            def _():
                for g in (0, 1):
                    direct[4 * step + 2 * way + g][0].start()

    def block_of(down, right):
        return ds_ref[((line + down + LINES) % LINES) * COLS + (y + right) % COLS]

    def factors(mine, other):
        live = mine == other
        temper = scale_ref[mine] * LOG2E
        return jnp.where(live, temper, 0.0), jnp.where(live, 0.0, NEG)

    def video(b):
        return held[pl.ds(4 + 2 * b, 2)].reshape(BLK, D)

    def multiply(first, count, b, index):
        score[pl.ds(index, count)] = lax.dot_general(
            held[pl.ds(first, count)].reshape(count * HALF, D), video(b), (((1,), (1,)), ((), ())),
            preferred_element_type=F32).reshape(count, HALF, BLK)

    def fold(slot, blocks):
        def rows(c, tops):
            at_rows = pl.ds(pl.multiple_of(c * CH, CH), CH)
            parts, peaks = [], []
            for n, (b, index, mult, off) in enumerate(blocks):
                s = score[index, at_rows, :] * mult + off
                score[index, at_rows, :] = s
                peak = tops[n]
                for e in range(0, CH, 8):
                    peak = jnp.maximum(peak, s[e:e + 8])
                peaks.append(peak)
                parts.extend([s[:, 128 * q:128 * q + 128] for q in range(4)])
            top = parts[0]
            for part in parts[1:]:
                top = jnp.maximum(top, part)
            total = jnp.exp2(parts[0] - top)
            for part in parts[1:]:
                total = total + jnp.exp2(part - top)
            row_m[slot, at_rows, :] = top
            row_l[slot, at_rows, :] = total
            return tuple(peaks)

        old = [col_m[b] for b, _, _, _ in blocks]
        new = lax.fori_loop(0, HALF // CH, rows, tuple(old))

        def columns(c, sums):
            at_rows = pl.ds(pl.multiple_of(c * CH, CH), CH)
            result = []
            for n, (b, index, mult, off) in enumerate(blocks):
                s = score[index, at_rows, :]
                total = sums[n]
                for e in range(0, CH, 8):
                    total = total + jnp.exp2(s[e:e + 8] - new[n])
                result.append(total)
            return tuple(result)

        begin = tuple(col_l[b] * jnp.exp2(old[n] - new[n]) for n, (b, _, _, _) in enumerate(blocks))
        sums = lax.fori_loop(0, HALF // CH, columns, begin)
        for n, (b, _, _, _) in enumerate(blocks):
            col_m[b] = new[n]
            col_l[b] = sums[n]

    def tile_of(u, b):
        k = u ^ (u // 2)
        return (b, 4 * b + u) + factors(block_of(0, k), block_of((b == 2) * 1 - (b == 1) * 1, 0))

    for copy in waiting:
        copy.wait()
    for g in (0, 1):
        unit = t * (10 - 10 * g) + (1 - t) * (4 + g)
        arrived(held.at[unit], r_held.at[unit, 0])
    arrived(wts.at[1 - t], r_in.at[0])
    log_w = jnp.log(wts[0, :, pl.ds(pl.multiple_of(HALF * t, HALF), HALF)][0:1, :]) * LOG2E
    lp[2, 0:1, :] = log_w
    mp[1, 2:3, :] = jnp.log(wts[1][0:1, :]) * LOG2E

    multiply(0, 1, 0, 0)
    fold(0, [tile_of(0, 0)])

    give = edge & (block_of(0, edge_k) == block_of(2 * sgn, 0))
    for step in range(4):
        for unit, q in ((2, step), (1, 3 - step)):
            arrived(held.at[unit, part(q)], r_held.at[unit, q])
        if step == 2:
            for unit, h, way in ((2, 0, 1), (1, 1, -1)):
                go(rcopy(held.at[unit, half(h)], held.at[3, half(h)], s_held.at[h], r_held.at[3, h], at(t, 0, way)))
        q = step + sel * (3 - 2 * step)

        @pl.when(edge)
        def _():
            xs[part(q)] = jnp.where(give, held[edge_u, part(q), :], held[4 + t, part(q), :])

        unit = 4 + 2 * late_b + t
        edge_go(rcopy(xs.at[part(q)], held.at[unit, part(q)], s_held.at[4 + step], r_held.at[unit, q], at(t, sgn, 0)))

    def share(b, sem):
        unit = 4 + 2 * b + t
        for step in range(4):
            q = step if sem < 12 else step + sel * (3 - 2 * step)
            arrived(held.at[unit, part(q)], r_held.at[unit, q])
            go(rcopy(held.at[unit, part(q)], held.at[unit, part(q)], s_held.at[sem + step], r_held.at[unit, q], mate))

    def shared(b):
        unit = 4 + 2 * b + 1 - t
        for q in range(4):
            arrived(held.at[unit, part(q)], r_held.at[unit, q])

    share(edge_b, 8)
    shared(edge_b)

    multiply(1, 2, 0, 1)
    multiply(0, 3, edge_b, 4 * edge_b)
    fold(5, [tile_of(0, edge_b)])

    def early(u, carry):
        fold(u, [tile_of(u, 0), tile_of(u, edge_b)])
        return carry

    lax.fori_loop(1, 3, early, 0)
    share(late_b, 12)

    lane = lax.broadcasted_iota(jnp.int32, (HALF, 128), 1)

    def unite(u, slot):
        m, other = row_m[u], row_m[slot]
        top = jnp.maximum(m, other)
        row_l[u] = row_l[u] * jnp.exp2(m - top) + row_l[slot] * jnp.exp2(other - top)
        row_m[u] = top

    def pack_rows(u):
        m, l = row_m[u], row_l[u]
        top = jnp.max(m, axis=1, keepdims=True)
        total = jnp.sum(l * jnp.exp2(m - top), axis=1, keepdims=True)
        turned = jnp.where(lane == 0, top, total).T
        if u == 4:
            lp[3, 0:2, :] = turned[0:2, :]
        else:
            lp[0, u:u + 1, :] = turned[0:1, :]
            lp[1, u:u + 1, :] = turned[1:2, :]

    @pl.when(edge)
    def _():
        multiply(4 + 2 * late_b + t, 1, edge_b, 12)
        fold(4, [(edge_b, 12) + factors(block_of(-sgn, edge_k), block_of(sgn, 0))])
        pack_rows(4)

    for c in range(COLS):
        edge_go(rcopy(lp.at[3], lx.at[sel], s_mid.at[c], r_mid.at[sel], at(t, -sgn, c)))
    for h in (0, 1):
        arrived(held.at[3, half(h)], r_held.at[3, h])
    multiply(3, 1, 0, 3)
    multiply(3, 1, edge_b, 4 * edge_b + 3)
    shared(late_b)
    multiply(0, 4, late_b, 4 * late_b)

    def late(u, carry):
        fold(6 + u, [tile_of(u, late_b)])
        return carry

    lax.fori_loop(0, 3, late, 0)

    fold(3, [tile_of(3, b) for b in (0, 1, 2)])
    for n, b in ((0, 1), (1, 0), (2, 2)):
        m, l = col_m[b], col_l[b]
        top = jnp.max(m, axis=0, keepdims=True)
        mp[n, 0:1, :] = top
        mp[n, 1:2, :] = jnp.sum(l * jnp.exp2(m - top), axis=0, keepdims=True)
    for way in (0, 1):
        for g in (0, 1):
            go(rcopy(mp.at[way:way + 2], m1.at[way, t], s_mid.at[4 + 2 * way + g], r_mid.at[2 + 2 * way + t],
                     at(g, 2 * way - 1, 0)))
            go(rcopy(mp.at[2 * way], m2.at[way, t], s_mid.at[8 + 2 * way + g], r_mid.at[6 + 2 * way + t],
                     at(g, 4 * way - 2, 0)))
    go(rcopy(mp, m3, s_mid.at[12], r_mid.at[10], mate))
    for u, slot in ((1, 7), (2, 8), (0, 5), (0, 6)):
        unite(u, slot)
    for u in range(4):
        pack_rows(u)
    go(rcopy(lp.at[0:3], lq.at[y], s_mid.at[16], r_mid.at[14 + y], at(t, 1, COLS - y)))
    go(rcopy(lp.at[0:3], lq.at[y], s_mid.at[17], r_mid.at[14 + y], at(t, -1, COLS - 1 - y)))
    for k in (2, 1, 3):
        go(rcopy(lp.at[0:3], li.at[k - 1], s_mid.at[12 + k], r_mid.at[10 + k], at(t, 0, k)))

    def merge(parts):
        tops = [m for m, _ in parts]
        top = tops[0]
        for other in tops[1:]:
            top = jnp.maximum(top, other)
        total = parts[0][1] * jnp.exp2(tops[0] - top)
        for n in range(1, len(parts)):
            total = total + parts[n][1] * jnp.exp2(tops[n] - top)
        return top + jnp.log(total) * LOG2E

    for way in (0, 1):
        arrived(lx.at[way], r_mid.at[way])
        for g in (0, 1):
            arrived(m1.at[way, g], r_mid.at[2 + 2 * way + g])
            arrived(m2.at[way, g], r_mid.at[6 + 2 * way + g])
    arrived(m3, r_mid.at[10])

    def pair(ref, *index):
        return ref[index + (slice(0, 1),)], ref[index + (slice(1, 2),)]

    both = (0, 1)
    mf[0] = merge([pair(mp, 1), pair(m3, 1)] + [pair(m1, 0, g, 0) for g in both] + [pair(m1, 1, g, 1) for g in both]
                  ) - mp[1, 2:3, :]
    mf[1] = merge([pair(mp, 0), pair(m3, 0)] + [pair(m1, 1, g, 0) for g in both] + [pair(m2, 1, g) for g in both]
                  ) - m1[1, 0, 0, 2:3, :]
    mf[2] = merge([pair(mp, 2), pair(m3, 2)] + [pair(m1, 0, g, 1) for g in both] + [pair(m2, 0, g) for g in both]
                  ) - m1[0, 0, 1, 2:3, :]
    for k in (1, 2, 3):
        arrived(li.at[k - 1], r_mid.at[10 + k])

    def line_of(ref, n):
        return ref[0, n:n + 1, :], ref[1, n:n + 1, :]

    def far_part(column):
        m = jnp.where(column == 3, lx[0, 0:1, :], jnp.where(column == 0, lx[1, 0:1, :], NEG))
        l = jnp.where(column == 3, lx[0, 1:2, :], jnp.where(column == 0, lx[1, 1:2, :], 0.0))
        return m, l

    for u in range(4):
        k = u ^ (u // 2)
        parts = [line_of(lp, u), far_part((y + k) % COLS)]
        for other in (1, 2, 3):
            theirs = (k - other) % 4
            parts.append(line_of(li.at[3 - other], theirs ^ (theirs // 2)))
        lf[u] = merge(parts) - (lp[2, 0:1, :] if k == 0 else li[3 - k, 2, 0:1, :])

    def turn(u):
        lcol[u] = jnp.broadcast_to(lf[u], (128, HALF)).T

    for u in range(4):
        turn(u)

    def turn_far():
        parts = [(lp[3, 0:1, :], lp[3, 1:2, :])]
        for c in range(COLS):
            arrived(lq.at[c], r_mid.at[14 + c])
            one, two = (k ^ (k // 2) for k in ((3 - c) % 4, (0 - c) % 4))
            parts.append(tuple(jnp.where(sel == 0, lq[c, n, one:one + 1, :], lq[c, n, two:two + 1, :])
                               for n in (0, 1)))
        lf[4] = merge(parts) - jnp.where(sel == 0, lq[3, 2, 0:1, :], lq[0, 2, 0:1, :])
        turn(4)

    def derive(slot, blocks, diagonal=False):
        cols = [jnp.broadcast_to(mf[b], (CH, BLK)) for b, _ in blocks]

        def rows(c, carry):
            at_rows = pl.ds(pl.multiple_of(c * CH, CH), CH)
            lse = jnp.concatenate([lcol[slot, at_rows, :]] * 4, axis=1)
            for n, (b, index) in enumerate(blocks):
                s = score[index, at_rows, :]
                g = jnp.exp2(s - lse) + jnp.exp2(s - cols[n])
                if diagonal:
                    r_id = lax.broadcasted_iota(jnp.int32, (CH, BLK), 0) + c * CH + HALF * t
                    c_id = lax.broadcasted_iota(jnp.int32, (CH, BLK), 1)
                    both = jnp.broadcast_to(wts[0][0:1, :] + wts[1][0:1, :], (CH, BLK))
                    g = g - jnp.where(r_id == c_id, both, 0.0)
                mass[index, at_rows, :] = g.astype(BF16)
            return carry

        lax.fori_loop(0, HALF // CH, rows, 0)

    def derive_units(first, last, blocks):
        def one(u, carry):
            derive(u, [(b, 4 * b + u) for b in blocks])
            return carry

        lax.fori_loop(first, last, one, 0)

    def row_grad(first, count):
        def term(b):
            return jnp.dot(mass[4 * b + first:4 * b + first + count].reshape(count * HALF, BLK), video(b),
                           preferred_element_type=F32)

        return term(0) + term(1) + term(2)

    mine = pl.ds(pl.multiple_of(HALF * t, HALF), HALF)
    others = pl.ds(pl.multiple_of(HALF * (1 - t), HALF), HALF)

    def col_grad(b, rows, far=False):
        g = mass[pl.ds(4 * b, 4), :, rows].reshape(4 * HALF, HALF)
        a = held[0:4].reshape(4 * HALF, D)
        zf[b, rows] = lax.dot_general(g, a, (((0,), (0,)), ((), ())), preferred_element_type=F32)
        if far:
            @pl.when(edge)
            def _():
                zf[b, rows] += lax.dot_general(mass[12, :, rows], held[4 + 2 * late_b + t],
                                               (((0,), (0,)), ((), ())), preferred_element_type=F32)

    def hand_over(b, sem):
        go(rcopy(zf.at[b, others], zr.at[b], s_out.at[sem], r_out.at[sem], mate))

    def send_lines(b, sem, base, down, order):
        arrived(zr.at[b], r_out.at[sem])
        for step in range(4):
            q = step + order * (3 - 2 * step)
            mine_q = pl.ds(pl.multiple_of(HALF * t + PART * q, PART), PART)
            zo[b - 1, part(q)] = (zf[b, mine_q] + zr[b, part(q)]).astype(BF16)
            go(rcopy(zo.at[b - 1, part(q)], zi.at[b - 1, part(q)], s_z.at[base, q], r_z.at[b - 1, q],
                     at(t, down, 0)))

    derive_units(0, 4, (late_b,))
    col_grad(late_b, others)
    hand_over(late_b, 5)
    derive_units(3, 4, (0, edge_b))
    yt[...] = row_grad(3, 1).astype(BF16)
    for h, way in ((0, 1), (1, -1)):
        go(rcopy(yt.at[half(h)], yr.at[h], s_out.at[2 + h], r_out.at[2 + h], at(t, 0, way)))
    col_grad(late_b, mine)

    @pl.when(edge)
    def _():
        turn_far()
        derive(4, [(edge_b, 12)])
        zf[late_b, mine] += jnp.dot(mass[12], video(edge_b), preferred_element_type=F32)

    send_lines(late_b, 5, 0, -sgn, sel)
    derive_units(0, 3, (edge_b,))
    col_grad(edge_b, others, True)
    hand_over(edge_b, 6)
    derive(0, [(0, 0)], True)
    derive_units(1, 3, (0,))
    yp[...] = row_grad(1, 2).reshape(2, HALF, D)
    early_parts = {}
    for step in (0, 1):
        for n, q in ((0, 3 - step), (1, step)):
            copy = rcopy(yo.at[n, part(q)], yi.at[n, part(q)], s_y.at[n, q], r_y.at[n, q], at(t, 0, 1 - 2 * n))
            early_parts[n, q] = copy
            pending.append(copy)

            @pl.when(jnp.logical_not(edge & (sel == 1 - n)))
            def _():
                yo[n, part(q)] = yp[n, part(q)].astype(BF16)
                copy.start()
    col_grad(edge_b, mine, True)
    send_lines(edge_b, 6, 1, sgn, 1 - sel)

    for step in range(4):
        q = step + sel * (3 - 2 * step)

        @pl.when(edge)
        def _():
            arrived(zi.at[sel, part(q)], r_z.at[sel, q])
            yp[1 - sel, part(q)] += jnp.where(give, zi[sel, part(q), :].astype(F32), 0.0)

        if step == 2:
            for n in (0, 1):
                arrived(yr.at[n], r_out.at[2 + n])
                yp[n, half(n)] += yr[n].astype(F32)
        for n, q in ((0, 3 - step), (1, step)):
            if step < 2:
                @pl.when(edge & (sel == 1 - n))
                def _():
                    yo[n, part(q)] = yp[n, part(q)].astype(BF16)
                    early_parts[n, q].start()
            else:
                yo[n, part(q)] = yp[n, part(q)].astype(BF16)
                go(rcopy(yo.at[n, part(q)], yi.at[n, part(q)], s_y.at[n, q], r_y.at[n, q], at(t, 0, 1 - 2 * n)))

    col_grad(0, others)
    hand_over(0, 4)
    col_grad(0, mine)
    ya[...] = row_grad(0, 1)

    temper = scale_ref[block_of(0, 0)]
    home, away = [], []
    for q in range(4):
        to = out_ref.at[0, pl.ds(pl.multiple_of(HALF * t + PART * q, PART), PART)]
        home.append(pltpu.make_async_copy(ends.at[t, part(q)], to, s_home.at[q]))
        away.append(rcopy(ends.at[1 - t, part(q)], to, s_away.at[q], r_away.at[q], mate))

    def finish(mode, q, value):
        ends[mode, part(q)] = temper * value

        @pl.when(t == mode)
        def _():
            home[q].start()

        @pl.when(t != mode)
        def _():
            away[q].start()

    arrived(zr.at[0], r_out.at[4])
    for q in (1, 2, 0, 3):
        rows = part(q)
        for n in (0, 1):
            arrived(yi.at[n, rows], r_y.at[n, q])
        finish(0, q, ya[rows, :] + yi[0, rows, :].astype(F32) + yi[1, rows, :].astype(F32))
        for j in (0, 1):
            @pl.when(jnp.logical_not(edge & (sel == j)))
            def _():
                arrived(zi.at[j, rows], r_z.at[j, q])

        mine_q = pl.ds(pl.multiple_of(HALF * t + PART * q, PART), PART)
        finish(1, q, (zf[0, mine_q, :] + zr[0, rows, :]
                      + jnp.where(give & (sel == 0), 0.0, zi[0, rows, :].astype(F32))
                      + jnp.where(give & (sel == 1), 0.0, zi[1, rows, :].astype(F32))))
    for q in range(4):
        home[q].wait()
        away[q].wait_send()
        to = out_ref.at[0, pl.ds(pl.multiple_of(HALF * (1 - t) + PART * q, PART), PART)]
        rcopy(to, to, s_away.at[q], r_away.at[q], mate).wait_recv()
    drain()


def on_device(embeddings, loss_weights, dataset_of_block, logit_scale):
    vmem = pl.BlockSpec(memory_space=pltpu.VMEM)
    smem = pl.BlockSpec(memory_space=pltpu.SMEM)
    hbm = pl.BlockSpec(memory_space=pl.ANY)
    dma = pltpu.SemaphoreType.DMA
    scratch = [
        pltpu.VMEM((UNITS, HALF, D), BF16),
        pltpu.VMEM((13, HALF, BLK), F32),
        pltpu.VMEM((13, HALF, BLK), BF16),
        pltpu.VMEM((2, 8, BLK), F32),
        pltpu.VMEM((9, HALF, 128), F32),
        pltpu.VMEM((9, HALF, 128), F32),
        pltpu.VMEM((3, 8, BLK), F32),
        pltpu.VMEM((3, 8, BLK), F32),
        pltpu.VMEM((4, 4, HALF), F32),
        pltpu.VMEM((3, 3, 4, HALF), F32),
        pltpu.VMEM((2, 4, HALF), F32),
        pltpu.VMEM((4, 3, 4, HALF), F32),
        pltpu.VMEM((5, 1, HALF), F32),
        pltpu.VMEM((5, HALF, 128), F32),
        pltpu.VMEM((3, 4, BLK), F32),
        pltpu.VMEM((2, 2, 2, 4, BLK), F32),
        pltpu.VMEM((2, 2, 4, BLK), F32),
        pltpu.VMEM((3, 4, BLK), F32),
        pltpu.VMEM((3, 1, BLK), F32),
        pltpu.VMEM((HALF, D), F32),
        pltpu.VMEM((2, HALF, D), F32),
        pltpu.VMEM((2, HALF, D), BF16),
        pltpu.VMEM((2, HALF, D), BF16),
        pltpu.VMEM((HALF, D), BF16),
        pltpu.VMEM((2, HALF // 2, D), BF16),
        pltpu.VMEM((HALF, D), BF16),
        pltpu.VMEM((3, BLK, D), F32),
        pltpu.VMEM((3, HALF, D), F32),
        pltpu.VMEM((2, HALF, D), BF16),
        pltpu.VMEM((2, HALF, D), BF16),
        pltpu.VMEM((2, HALF, D), F32),
        dma((21,)), dma((1,)), dma((16,)), dma((UNITS, 4)), dma((18,)), dma((18,)), dma((14,)), dma((14,)),
        dma((2, 4)), dma((2, 4)), dma((2, 4)), dma((2, 4)), dma((4,)), dma((4,)), dma((4,)),
    ]
    return pl.pallas_call(
        kernel,
        out_shape=jax.ShapeDtypeStruct((1, BLK, D), F32),
        in_specs=[smem, smem, hbm, vmem],
        out_specs=hbm,
        scratch_shapes=scratch,
        compiler_params=pltpu.CompilerParams(
            collective_id=0, has_side_effects=True, vmem_limit_bytes=56 * 2**20),
    )(dataset_of_block, logit_scale, embeddings, loss_weights)


def solution(mesh):
    in_specs = (P("tower", "tile", None), P("tower", "tile"), P(), P())
    return jax.shard_map(
        on_device, mesh=mesh, in_specs=in_specs, out_specs=P("tower", "tile", None), check_vma=False)
```

```python
import jax
import jax.numpy as jnp
from jax import lax
from jax.experimental import pallas as pl
from jax.experimental.pallas import tpu as pltpu
from jax.sharding import PartitionSpec as P


MESH = pl.DeviceIdType.MESH
F32, BF16 = jnp.float32, jnp.bfloat16
BLK, D = 512, 1024
HALF, PART = BLK // 2, BLK // 8
COLS, LINES = 4, 32
NEG = -1e30
LOG2E = 1.4426950408889634
CH = 64

UNITS = 11


def kernel(ds_ref, scale_ref, x_ref, wt_ref, out_ref, held, score, mass, wts,
           row_m, row_l, col_m, col_l, lp, li, lx, lq, lf, lcol, mp, m1, m2, m3, mf,
           ya, yp, yo, yi, yt, yr, xs, zf, zr, zo, zi, ends,
           s_in, r_in, s_held, r_held, s_mid, r_mid, s_out, r_out, s_y, r_y, s_z, r_z, s_home, s_away, r_away):
    t = lax.axis_index("tower")
    tile = lax.axis_index("tile")
    line, y = tile // COLS, tile % COLS
    sel = y // 2
    sgn = 1 - 2 * sel
    edge = y % 3 == 0
    edge_k = 3 - 2 * sel
    edge_u = 2 - sel
    edge_b = 2 - sel
    late_b = 1 + sel

    def at(core, down, right):
        return (core, ((line + down + LINES) % LINES) * COLS + (y + right) % COLS)

    def rcopy(src, dst, ss, rs, dev):
        return pltpu.make_async_remote_copy(
            src_ref=src, dst_ref=dst, send_sem=ss, recv_sem=rs, device_id=dev, device_id_type=MESH)

    mate = at(1 - t, 0, 0)

    def arrived(ref, sem):
        rcopy(ref, ref, sem, sem, mate).wait_recv()

    barrier = pltpu.get_barrier_semaphore()
    peers = [mate, at(t, 0, 2)]
    for core in (0, 1):
        for k in (1, 3):
            peers.append(at(core, 0, k))
        for dz in (1, -1, 2, -2):
            peers.append(at(core, dz, 0))
    peers.append(at(t, 1, COLS - y))
    peers.append(at(t, -1, COLS - 1 - y))
    for dev in peers:
        pl.semaphore_signal(barrier, inc=1, device_id=dev, device_id_type=MESH)

    @pl.when(edge)
    def _():
        for c in range(COLS):
            pl.semaphore_signal(barrier, inc=1, device_id=at(t, -sgn, c), device_id_type=MESH)

    waiting = []
    for g in (0, 1):
        own = (1 - t) * (10 * g) + t * (4 + g)
        waiting.append(pltpu.make_async_copy(x_ref.at[0, pl.ds(HALF * g, HALF)], held.at[own], s_in.at[19 + g]))
        waiting[-1].start()
    wts[t] = jnp.broadcast_to(wt_ref[...].astype(F32), (8, BLK))
    col_m[...] = jnp.full(col_m.shape, NEG, F32)
    col_l[...] = jnp.zeros(col_l.shape, F32)
    row_m[4] = jnp.full((HALF, 128), NEG, F32)
    row_l[4] = jnp.zeros((HALF, 128), F32)
    pl.semaphore_wait(barrier, len(peers) + COLS * edge.astype(jnp.int32))

    pending, edge_pending = [], []

    def go(copy):
        copy.start()
        pending.append(copy)

    def edge_go(copy):
        edge_pending.append(copy)

        @pl.when(edge)
        def _():
            copy.start()

    def drain():
        for copy in pending:
            copy.wait_send()
        for step in range(4):
            for way in (0, 1):
                @pl.when(jnp.logical_not(direct[4 * step + 2 * way][1]))
                def _():
                    for g in (0, 1):
                        direct[4 * step + 2 * way + g][0].wait_send()

        @pl.when(edge)
        def _():
            for copy in edge_pending:
                copy.wait_send()

    def half(h):
        return pl.ds(HALF // 2 * h, HALF // 2)

    def part(q):
        return pl.ds(PART * q if isinstance(q, int) else pl.multiple_of(PART * q, PART), PART)

    direct = []
    for step in range(4):
        for way in (0, 1):
            q = step if way == 0 else 3 - step
            held_back = edge & (sel == way) & (t == 1)
            for g in (0, 1):
                sign = 1 - 2 * way
                unit = (1 - t) * (2 - way) + t * (6 + 2 * way + g)
                copy = rcopy(x_ref.at[0, pl.ds(HALF * g + PART * q, PART)], held.at[unit, part(q)],
                             s_in.at[4 * step + 2 * way + g], r_held.at[unit, q], at(g, t * sign, (1 - t) * sign))
                direct.append((copy, held_back))

    for g in (0, 1):
        unit = (1 - t) * (10 - 10 * g) + t * (4 + g)
        go(rcopy(x_ref.at[0, pl.ds(HALF * g, HALF)], held.at[unit], s_in.at[16 + g], r_held.at[unit, 0], mate))
    go(rcopy(wts.at[t], wts.at[t], s_in.at[18], r_in.at[0], mate))
    for step in range(4):
        for way in (0, 1):
            @pl.when(jnp.logical_not(direct[4 * step + 2 * way][1]))
            def _():
                for g in (0, 1):
                    direct[4 * step + 2 * way + g][0].start()

    def block_of(down, right):
        return ds_ref[((line + down + LINES) % LINES) * COLS + (y + right) % COLS]

    def factors(mine, other):
        live = mine == other
        temper = scale_ref[mine] * LOG2E
        return jnp.where(live, temper, 0.0), jnp.where(live, 0.0, NEG)

    def video(b):
        return held[pl.ds(4 + 2 * b, 2)].reshape(BLK, D)

    def multiply(first, count, b, index):
        score[pl.ds(index, count)] = lax.dot_general(
            held[pl.ds(first, count)].reshape(count * HALF, D), video(b), (((1,), (1,)), ((), ())),
            preferred_element_type=F32).reshape(count, HALF, BLK)

    def fold(slot, blocks):
        ch = 2 * CH if len(blocks) < 3 else CH
        def rows(c, tops):
            at_rows = pl.ds(pl.multiple_of(c * ch, ch), ch)
            parts, peaks = [], []
            for n, (b, index, mult, off) in enumerate(blocks):
                s = score[index, at_rows, :] * mult + off
                score[index, at_rows, :] = s
                peak = tops[n]
                for e in range(0, ch, 8):
                    peak = jnp.maximum(peak, s[e:e + 8])
                peaks.append(peak)
                parts.extend([s[:, 128 * q:128 * q + 128] for q in range(4)])
            top = parts[0]
            for part in parts[1:]:
                top = jnp.maximum(top, part)
            total = jnp.exp2(parts[0] - top)
            for part in parts[1:]:
                total = total + jnp.exp2(part - top)
            row_m[slot, at_rows, :] = top
            row_l[slot, at_rows, :] = total
            return tuple(peaks)

        old = [col_m[b] for b, _, _, _ in blocks]
        new = lax.fori_loop(0, HALF // ch, rows, tuple(old))

        def columns(c, sums):
            at_rows = pl.ds(pl.multiple_of(c * ch, ch), ch)
            result = []
            for n, (b, index, mult, off) in enumerate(blocks):
                s = score[index, at_rows, :]
                total = sums[n]
                for e in range(0, ch, 8):
                    total = total + jnp.exp2(s[e:e + 8] - new[n])
                result.append(total)
            return tuple(result)

        begin = tuple(col_l[b] * jnp.exp2(old[n] - new[n]) for n, (b, _, _, _) in enumerate(blocks))
        sums = lax.fori_loop(0, HALF // ch, columns, begin)
        for n, (b, _, _, _) in enumerate(blocks):
            col_m[b] = new[n]
            col_l[b] = sums[n]

    def tile_of(u, b):
        k = u ^ (u // 2)
        return (b, 4 * b + u) + factors(block_of(0, k), block_of((b == 2) * 1 - (b == 1) * 1, 0))

    for copy in waiting:
        copy.wait()
    for g in (0, 1):
        unit = t * (10 - 10 * g) + (1 - t) * (4 + g)
        arrived(held.at[unit], r_held.at[unit, 0])
    arrived(wts.at[1 - t], r_in.at[0])
    log_w = jnp.log(wts[0, :, pl.ds(pl.multiple_of(HALF * t, HALF), HALF)][0:1, :]) * LOG2E
    lp[2, 0:1, :] = log_w
    mp[1, 2:3, :] = jnp.log(wts[1][0:1, :]) * LOG2E

    multiply(0, 1, 0, 0)
    fold(0, [tile_of(0, 0)])

    give = edge & (block_of(0, edge_k) == block_of(2 * sgn, 0))
    for step in range(4):
        for unit, q in ((2, step), (1, 3 - step)):
            arrived(held.at[unit, part(q)], r_held.at[unit, q])
        if step == 2:
            for unit, h, way in ((2, 0, 1), (1, 1, -1)):
                go(rcopy(held.at[unit, half(h)], held.at[3, half(h)], s_held.at[h], r_held.at[3, h], at(t, 0, way)))
        q = step + sel * (3 - 2 * step)

        @pl.when(edge)
        def _():
            xs[part(q)] = jnp.where(give, held[edge_u, part(q), :], held[4 + t, part(q), :])

        unit = 4 + 2 * late_b + t
        edge_go(rcopy(xs.at[part(q)], held.at[unit, part(q)], s_held.at[4 + step], r_held.at[unit, q], at(t, sgn, 0)))

    def share(b, sem):
        unit = 4 + 2 * b + t
        for step in range(4):
            q = step if sem < 12 else step + sel * (3 - 2 * step)
            arrived(held.at[unit, part(q)], r_held.at[unit, q])
            go(rcopy(held.at[unit, part(q)], held.at[unit, part(q)], s_held.at[sem + step], r_held.at[unit, q], mate))

    def shared(b):
        unit = 4 + 2 * b + 1 - t
        for q in range(4):
            arrived(held.at[unit, part(q)], r_held.at[unit, q])

    share(edge_b, 8)
    shared(edge_b)

    multiply(1, 2, 0, 1)
    multiply(0, 3, edge_b, 4 * edge_b)
    fold(5, [tile_of(0, edge_b)])

    def early(u, carry):
        fold(u, [tile_of(u, 0), tile_of(u, edge_b)])
        return carry

    lax.fori_loop(1, 3, early, 0)
    share(late_b, 12)

    lane = lax.broadcasted_iota(jnp.int32, (HALF, 128), 1)

    def unite(u, slot):
        m, other = row_m[u], row_m[slot]
        top = jnp.maximum(m, other)
        row_l[u] = row_l[u] * jnp.exp2(m - top) + row_l[slot] * jnp.exp2(other - top)
        row_m[u] = top

    def pack_rows(u):
        m, l = row_m[u], row_l[u]
        top = jnp.max(m, axis=1, keepdims=True)
        total = jnp.sum(l * jnp.exp2(m - top), axis=1, keepdims=True)
        turned = jnp.where(lane == 0, top, total).T
        if u == 4:
            lp[3, 0:2, :] = turned[0:2, :]
        else:
            lp[0, u:u + 1, :] = turned[0:1, :]
            lp[1, u:u + 1, :] = turned[1:2, :]

    @pl.when(edge)
    def _():
        multiply(4 + 2 * late_b + t, 1, edge_b, 12)
        fold(4, [(edge_b, 12) + factors(block_of(-sgn, edge_k), block_of(sgn, 0))])
        pack_rows(4)

    for c in range(COLS):
        edge_go(rcopy(lp.at[3], lx.at[sel], s_mid.at[c], r_mid.at[sel], at(t, -sgn, c)))
    for h in (0, 1):
        arrived(held.at[3, half(h)], r_held.at[3, h])
    multiply(3, 1, 0, 3)
    multiply(3, 1, edge_b, 4 * edge_b + 3)
    shared(late_b)
    multiply(0, 4, late_b, 4 * late_b)

    def late(u, carry):
        fold(6 + u, [tile_of(u, late_b)])
        return carry

    lax.fori_loop(0, 3, late, 0)

    fold(3, [tile_of(3, b) for b in (0, 1, 2)])
    for n, b in ((0, 1), (1, 0), (2, 2)):
        m, l = col_m[b], col_l[b]
        top = jnp.max(m, axis=0, keepdims=True)
        mp[n, 0:1, :] = top
        mp[n, 1:2, :] = jnp.sum(l * jnp.exp2(m - top), axis=0, keepdims=True)
    for way in (0, 1):
        for g in (0, 1):
            go(rcopy(mp.at[way:way + 2], m1.at[way, t], s_mid.at[4 + 2 * way + g], r_mid.at[2 + 2 * way + t],
                     at(g, 2 * way - 1, 0)))
            go(rcopy(mp.at[2 * way], m2.at[way, t], s_mid.at[8 + 2 * way + g], r_mid.at[6 + 2 * way + t],
                     at(g, 4 * way - 2, 0)))
    go(rcopy(mp, m3, s_mid.at[12], r_mid.at[10], mate))
    for u, slot in ((1, 7), (2, 8), (0, 5), (0, 6)):
        unite(u, slot)
    for u in range(4):
        pack_rows(u)
    go(rcopy(lp.at[0:3], lq.at[y], s_mid.at[16], r_mid.at[14 + y], at(t, 1, COLS - y)))
    go(rcopy(lp.at[0:3], lq.at[y], s_mid.at[17], r_mid.at[14 + y], at(t, -1, COLS - 1 - y)))
    for k in (2, 1, 3):
        go(rcopy(lp.at[0:3], li.at[k - 1], s_mid.at[12 + k], r_mid.at[10 + k], at(t, 0, k)))

    def merge(parts):
        tops = [m for m, _ in parts]
        top = tops[0]
        for other in tops[1:]:
            top = jnp.maximum(top, other)
        total = parts[0][1] * jnp.exp2(tops[0] - top)
        for n in range(1, len(parts)):
            total = total + parts[n][1] * jnp.exp2(tops[n] - top)
        return top + jnp.log(total) * LOG2E

    for way in (0, 1):
        arrived(lx.at[way], r_mid.at[way])
        for g in (0, 1):
            arrived(m1.at[way, g], r_mid.at[2 + 2 * way + g])
            arrived(m2.at[way, g], r_mid.at[6 + 2 * way + g])
    arrived(m3, r_mid.at[10])

    def pair(ref, *index):
        return ref[index + (slice(0, 1),)], ref[index + (slice(1, 2),)]

    both = (0, 1)
    mf[0] = merge([pair(mp, 1), pair(m3, 1)] + [pair(m1, 0, g, 0) for g in both] + [pair(m1, 1, g, 1) for g in both]
                  ) - mp[1, 2:3, :]
    mf[1] = merge([pair(mp, 0), pair(m3, 0)] + [pair(m1, 1, g, 0) for g in both] + [pair(m2, 1, g) for g in both]
                  ) - m1[1, 0, 0, 2:3, :]
    mf[2] = merge([pair(mp, 2), pair(m3, 2)] + [pair(m1, 0, g, 1) for g in both] + [pair(m2, 0, g) for g in both]
                  ) - m1[0, 0, 1, 2:3, :]
    for k in (1, 2, 3):
        arrived(li.at[k - 1], r_mid.at[10 + k])

    def line_of(ref, n):
        return ref[0, n:n + 1, :], ref[1, n:n + 1, :]

    def far_part(column):
        m = jnp.where(column == 3, lx[0, 0:1, :], jnp.where(column == 0, lx[1, 0:1, :], NEG))
        l = jnp.where(column == 3, lx[0, 1:2, :], jnp.where(column == 0, lx[1, 1:2, :], 0.0))
        return m, l

    for u in range(4):
        k = u ^ (u // 2)
        parts = [line_of(lp, u), far_part((y + k) % COLS)]
        for other in (1, 2, 3):
            theirs = (k - other) % 4
            parts.append(line_of(li.at[3 - other], theirs ^ (theirs // 2)))
        lf[u] = merge(parts) - (lp[2, 0:1, :] if k == 0 else li[3 - k, 2, 0:1, :])

    def turn(u):
        lcol[u] = jnp.broadcast_to(lf[u], (128, HALF)).T

    for u in range(4):
        turn(u)

    def turn_far():
        parts = [(lp[3, 0:1, :], lp[3, 1:2, :])]
        for c in range(COLS):
            arrived(lq.at[c], r_mid.at[14 + c])
            one, two = (k ^ (k // 2) for k in ((3 - c) % 4, (0 - c) % 4))
            parts.append(tuple(jnp.where(sel == 0, lq[c, n, one:one + 1, :], lq[c, n, two:two + 1, :])
                               for n in (0, 1)))
        lf[4] = merge(parts) - jnp.where(sel == 0, lq[3, 2, 0:1, :], lq[0, 2, 0:1, :])
        turn(4)

    def derive(slot, blocks, diagonal=False):
        ch = 2 * CH if len(blocks) < 3 else CH
        cols = [jnp.broadcast_to(mf[b], (ch, BLK)) for b, _ in blocks]

        def rows(c, carry):
            at_rows = pl.ds(pl.multiple_of(c * ch, ch), ch)
            lse = jnp.concatenate([lcol[slot, at_rows, :]] * 4, axis=1)
            for n, (b, index) in enumerate(blocks):
                s = score[index, at_rows, :]
                g = jnp.exp2(s - lse) + jnp.exp2(s - cols[n])
                if diagonal:
                    r_id = lax.broadcasted_iota(jnp.int32, (ch, BLK), 0) + c * ch + HALF * t
                    c_id = lax.broadcasted_iota(jnp.int32, (ch, BLK), 1)
                    both = jnp.broadcast_to(wts[0][0:1, :] + wts[1][0:1, :], (ch, BLK))
                    g = g - jnp.where(r_id == c_id, both, 0.0)
                mass[index, at_rows, :] = g.astype(BF16)
            return carry

        lax.fori_loop(0, HALF // ch, rows, 0)

    def derive_units(first, last, blocks):
        def one(u, carry):
            derive(u, [(b, 4 * b + u) for b in blocks])
            return carry

        lax.fori_loop(first, last, one, 0)

    def row_grad(first, count):
        def term(b):
            return jnp.dot(mass[4 * b + first:4 * b + first + count].reshape(count * HALF, BLK), video(b),
                           preferred_element_type=F32)

        return term(0) + term(1) + term(2)

    mine = pl.ds(pl.multiple_of(HALF * t, HALF), HALF)
    others = pl.ds(pl.multiple_of(HALF * (1 - t), HALF), HALF)

    def col_grad(b, rows, far=False):
        g = mass[pl.ds(4 * b, 4), :, rows].reshape(4 * HALF, HALF)
        a = held[0:4].reshape(4 * HALF, D)
        zf[b, rows] = lax.dot_general(g, a, (((0,), (0,)), ((), ())), preferred_element_type=F32)
        if far:
            @pl.when(edge)
            def _():
                zf[b, rows] += lax.dot_general(mass[12, :, rows], held[4 + 2 * late_b + t],
                                               (((0,), (0,)), ((), ())), preferred_element_type=F32)

    def hand_over(b, sem):
        go(rcopy(zf.at[b, others], zr.at[b], s_out.at[sem], r_out.at[sem], mate))

    def send_lines(b, sem, base, down, order):
        arrived(zr.at[b], r_out.at[sem])
        for step in range(4):
            q = step + order * (3 - 2 * step)
            mine_q = pl.ds(pl.multiple_of(HALF * t + PART * q, PART), PART)
            zo[b - 1, part(q)] = (zf[b, mine_q] + zr[b, part(q)]).astype(BF16)
            go(rcopy(zo.at[b - 1, part(q)], zi.at[b - 1, part(q)], s_z.at[base, q], r_z.at[b - 1, q],
                     at(t, down, 0)))

    derive_units(0, 4, (late_b,))
    col_grad(late_b, others)
    hand_over(late_b, 5)
    derive_units(3, 4, (0, edge_b))
    yt[...] = row_grad(3, 1).astype(BF16)
    for h, way in ((0, 1), (1, -1)):
        go(rcopy(yt.at[half(h)], yr.at[h], s_out.at[2 + h], r_out.at[2 + h], at(t, 0, way)))
    col_grad(late_b, mine)

    @pl.when(edge)
    def _():
        turn_far()
        derive(4, [(edge_b, 12)])
        zf[late_b, mine] += jnp.dot(mass[12], video(edge_b), preferred_element_type=F32)

    send_lines(late_b, 5, 0, -sgn, sel)
    derive_units(0, 3, (edge_b,))
    col_grad(edge_b, others, True)
    hand_over(edge_b, 6)
    derive(0, [(0, 0)], True)
    derive_units(1, 3, (0,))
    yp[...] = row_grad(1, 2).reshape(2, HALF, D)
    early_parts = {}
    for step in (0, 1):
        for n, q in ((0, 3 - step), (1, step)):
            copy = rcopy(yo.at[n, part(q)], yi.at[n, part(q)], s_y.at[n, q], r_y.at[n, q], at(t, 0, 1 - 2 * n))
            early_parts[n, q] = copy
            pending.append(copy)

            @pl.when(jnp.logical_not(edge & (sel == 1 - n)))
            def _():
                yo[n, part(q)] = yp[n, part(q)].astype(BF16)
                copy.start()
    col_grad(edge_b, mine, True)
    send_lines(edge_b, 6, 1, sgn, 1 - sel)

    for step in range(4):
        q = step + sel * (3 - 2 * step)

        @pl.when(edge)
        def _():
            arrived(zi.at[sel, part(q)], r_z.at[sel, q])
            yp[1 - sel, part(q)] += jnp.where(give, zi[sel, part(q), :].astype(F32), 0.0)

        if step == 2:
            for n in (0, 1):
                arrived(yr.at[n], r_out.at[2 + n])
                yp[n, half(n)] += yr[n].astype(F32)
        for n, q in ((0, 3 - step), (1, step)):
            if step < 2:
                @pl.when(edge & (sel == 1 - n))
                def _():
                    yo[n, part(q)] = yp[n, part(q)].astype(BF16)
                    early_parts[n, q].start()
            else:
                yo[n, part(q)] = yp[n, part(q)].astype(BF16)
                go(rcopy(yo.at[n, part(q)], yi.at[n, part(q)], s_y.at[n, q], r_y.at[n, q], at(t, 0, 1 - 2 * n)))

    col_grad(0, others)
    hand_over(0, 4)
    col_grad(0, mine)
    ya[...] = row_grad(0, 1)

    temper = scale_ref[block_of(0, 0)]
    home, away = [], []
    for q in range(4):
        to = out_ref.at[0, pl.ds(pl.multiple_of(HALF * t + PART * q, PART), PART)]
        home.append(pltpu.make_async_copy(ends.at[t, part(q)], to, s_home.at[q]))
        away.append(rcopy(ends.at[1 - t, part(q)], to, s_away.at[q], r_away.at[q], mate))

    def finish(mode, q, value):
        ends[mode, part(q)] = temper * value

        @pl.when(t == mode)
        def _():
            home[q].start()

        @pl.when(t != mode)
        def _():
            away[q].start()

    arrived(zr.at[0], r_out.at[4])
    for q in (1, 2, 0, 3):
        rows = part(q)
        for n in (0, 1):
            arrived(yi.at[n, rows], r_y.at[n, q])
        finish(0, q, ya[rows, :] + yi[0, rows, :].astype(F32) + yi[1, rows, :].astype(F32))
        for j in (0, 1):
            @pl.when(jnp.logical_not(edge & (sel == j)))
            def _():
                arrived(zi.at[j, rows], r_z.at[j, q])

        mine_q = pl.ds(pl.multiple_of(HALF * t + PART * q, PART), PART)
        finish(1, q, (zf[0, mine_q, :] + zr[0, rows, :]
                      + jnp.where(give & (sel == 0), 0.0, zi[0, rows, :].astype(F32))
                      + jnp.where(give & (sel == 1), 0.0, zi[1, rows, :].astype(F32))))
    for q in range(4):
        home[q].wait()
        away[q].wait_send()
        to = out_ref.at[0, pl.ds(pl.multiple_of(HALF * (1 - t) + PART * q, PART), PART)]
        rcopy(to, to, s_away.at[q], r_away.at[q], mate).wait_recv()
    drain()


def on_device(embeddings, loss_weights, dataset_of_block, logit_scale):
    vmem = pl.BlockSpec(memory_space=pltpu.VMEM)
    smem = pl.BlockSpec(memory_space=pltpu.SMEM)
    hbm = pl.BlockSpec(memory_space=pl.ANY)
    dma = pltpu.SemaphoreType.DMA
    scratch = [
        pltpu.VMEM((UNITS, HALF, D), BF16),
        pltpu.VMEM((13, HALF, BLK), F32),
        pltpu.VMEM((13, HALF, BLK), BF16),
        pltpu.VMEM((2, 8, BLK), F32),
        pltpu.VMEM((9, HALF, 128), F32),
        pltpu.VMEM((9, HALF, 128), F32),
        pltpu.VMEM((3, 8, BLK), F32),
        pltpu.VMEM((3, 8, BLK), F32),
        pltpu.VMEM((4, 4, HALF), F32),
        pltpu.VMEM((3, 3, 4, HALF), F32),
        pltpu.VMEM((2, 4, HALF), F32),
        pltpu.VMEM((4, 3, 4, HALF), F32),
        pltpu.VMEM((5, 1, HALF), F32),
        pltpu.VMEM((5, HALF, 128), F32),
        pltpu.VMEM((3, 4, BLK), F32),
        pltpu.VMEM((2, 2, 2, 4, BLK), F32),
        pltpu.VMEM((2, 2, 4, BLK), F32),
        pltpu.VMEM((3, 4, BLK), F32),
        pltpu.VMEM((3, 1, BLK), F32),
        pltpu.VMEM((HALF, D), F32),
        pltpu.VMEM((2, HALF, D), F32),
        pltpu.VMEM((2, HALF, D), BF16),
        pltpu.VMEM((2, HALF, D), BF16),
        pltpu.VMEM((HALF, D), BF16),
        pltpu.VMEM((2, HALF // 2, D), BF16),
        pltpu.VMEM((HALF, D), BF16),
        pltpu.VMEM((3, BLK, D), F32),
        pltpu.VMEM((3, HALF, D), F32),
        pltpu.VMEM((2, HALF, D), BF16),
        pltpu.VMEM((2, HALF, D), BF16),
        pltpu.VMEM((2, HALF, D), F32),
        dma((21,)), dma((1,)), dma((16,)), dma((UNITS, 4)), dma((18,)), dma((18,)), dma((14,)), dma((14,)),
        dma((2, 4)), dma((2, 4)), dma((2, 4)), dma((2, 4)), dma((4,)), dma((4,)), dma((4,)),
    ]
    return pl.pallas_call(
        kernel,
        out_shape=jax.ShapeDtypeStruct((1, BLK, D), F32),
        in_specs=[smem, smem, hbm, vmem],
        out_specs=hbm,
        scratch_shapes=scratch,
        compiler_params=pltpu.CompilerParams(
            collective_id=0, has_side_effects=True, vmem_limit_bytes=56 * 2**20),
    )(dataset_of_block, logit_scale, embeddings, loss_weights)


def solution(mesh):
    in_specs = (P("tower", "tile", None), P("tower", "tile"), P(), P())
    return jax.shard_map(
        on_device, mesh=mesh, in_specs=in_specs, out_specs=P("tower", "tile", None), check_vma=False)
```
